512 devices in a mesh: rows: 64 (over z, y), cols: 8 (over x, core).
Axes of the slice: x: 4, y: 4, z: 16, core: 2. Of those that a mesh axis runs over, the one named last changes fastest.
Arguments:
- snapshots: bfloat16 [131072, 2048], P('rows', 'cols')
- orient: int32 [3, 8], P(None, 'cols'), may hold values 0 or 1
Outputs:
- rotated: bfloat16 [131072, 2048], P('rows', 'cols')
- column_rms: float32 [2048], P('cols')
The draws below stay inside these ranges and needn't reach their ends.
All inputs are finite; a program needn't handle non-finite values. No bound on the sum of `orient` on one device may be relied on, other than what follows from the above.
Results may differ from the reference program's by a relative error of at most 0.011.
Values may be sent and summed in bfloat16 or wider, within the bound.
No kernel may reach another device: no remote copies, remote signals or barrier semaphores. Data moves between devices by JAX's collectives and lax.ppermute only.
A program may use at most 64 MiB of HBM per device.

```python
import math
import jax
import jax.numpy as jnp
from jax import lax

BLOCK = 128
ROUNDS = 3
POLAR_ITERS = 12
SNAP_ROWS = 131072
COLUMNS = 2048
N_COLS = 8


def draw_snapshots(key, part):
    key = jax.random.fold_in(key, 7)
    keys = jax.random.split(key, 7)
    noise = jax.random.normal(keys[0], (SNAP_ROWS, COLUMNS), jnp.float32)
    common = 0.7
    ceiling = math.log(10.0)
    left_mode = jax.random.normal(keys[1], (SNAP_ROWS, 1), jnp.float32)
    right_mode = jax.random.normal(keys[2], (SNAP_ROWS, 1), jnp.float32)
    left_weight = jax.random.normal(keys[3], (1, COLUMNS), jnp.float32)
    right_weight = jax.random.normal(keys[4], (1, COLUMNS), jnp.float32)
    column_scale = jnp.exp(jax.random.uniform(keys[5], (1, COLUMNS), jnp.float32, 0.0, ceiling))
    position = jnp.arange(SNAP_ROWS, dtype=jnp.float32)[:, None] / SNAP_ROWS
    row_scale = jnp.exp(math.log(3.0) * position) * jnp.exp(jax.random.uniform(keys[6], (SNAP_ROWS, 1), jnp.float32, -0.3, 0.3))
    left_amount = jnp.where(position < 0.25, 3.0, 0.3)
    right_amount = jnp.where(position < 0.5, 0.3, 1.0)
    modes = left_amount * left_mode * left_weight + right_amount * right_mode * right_weight
    values = row_scale * column_scale * (noise + common * modes)
    return values.astype(jnp.bfloat16)


def touch_ends(result, own_key, smallest, largest):
    index_at = [jax.random.randint(jax.random.fold_in(own_key, axis), (), 0, length) for axis, length in enumerate(result.shape)]
    widest = result.shape.index(max(result.shape))
    neighbour = index_at[:widest] + [(index_at[widest] + 1) % result.shape[widest]] + index_at[widest + 1:]
    return result.at[tuple(index_at)].set(smallest).at[tuple(neighbour)].set(largest)


def setup_inputs(seed: int = 0) -> dict:
    key_of = jax.random.split(jax.random.key(seed), 3)
    snapshots = draw_snapshots(jax.random.fold_in(key_of[2], 71), 0)
    orient = touch_ends((jax.random.randint(key_of[1], (ROUNDS, N_COLS), 0, 2) < 1).astype(jnp.int32), jax.random.fold_in(key_of[1], 1), 0, 1)
    return {"snapshots": snapshots, "orient": orient}


def inner(left, right):
    return lax.dot_general(left, right, (((0,), (0,)), ((), ())), preferred_element_type=jnp.float32)

def polar(gram):
    order = gram.shape[0]
    trace_mean = jnp.trace(gram) / order + 1e-06
    upper_part = jnp.triu(gram / trace_mean, 1)
    generator = upper_part - upper_part.T
    initial = jnp.eye(order, dtype=jnp.float32) + 0.5 * generator
    initial = initial / jnp.sqrt(jnp.sum(initial * initial))

    def refine(sweep, iterate):
        square = jnp.dot(iterate.T, iterate, precision=lax.Precision.HIGHEST)
        return 1.5 * iterate - 0.5 * jnp.dot(iterate, square, precision=lax.Precision.HIGHEST)
    return lax.fori_loop(0, POLAR_ITERS, refine, initial).astype(jnp.bfloat16)

def rotate_pair(paired):
    gram = inner(paired, paired)
    return jnp.dot(paired, polar(gram), preferred_element_type=jnp.float32).astype(jnp.bfloat16)

def reference(snapshots, orient):
    slots = snapshots.reshape(SNAP_ROWS, N_COLS, 2, BLOCK)
    upper_block = slots[:, :, 0, :].transpose(1, 0, 2)
    lower_block = slots[:, :, 1, :].transpose(1, 0, 2)
    for round_index in range(ROUNDS):
        flipped = (orient[round_index] == 1)[:, None, None]
        first = jnp.where(flipped, lower_block, upper_block)
        second = jnp.where(flipped, upper_block, lower_block)
        paired = jnp.concatenate([first, second], axis=2)
        turned = lax.map(rotate_pair, paired)
        first = turned[:, :, :BLOCK]
        second = turned[:, :, BLOCK:]
        upper_block = jnp.where(flipped, second, first)
        lower_block = jnp.where(flipped, first, second)
        if round_index + 1 < ROUNDS:
            upper_block, lower_block = (jnp.concatenate([upper_block[:1], lower_block[:1], upper_block[1:N_COLS - 1]], axis=0), jnp.concatenate([lower_block[1:], upper_block[N_COLS - 1:]], axis=0))
    stacked = jnp.stack([upper_block, lower_block], axis=2)
    rotated = stacked.transpose(1, 0, 2, 3).reshape(SNAP_ROWS, COLUMNS)
    wide = rotated.astype(jnp.float32)
    column_rms = jnp.sqrt(lax.optimization_barrier(jnp.sum(wide * wide, axis=0)) / SNAP_ROWS)
    return (rotated, column_rms)
```

```python
import functools

import jax
import jax.numpy as jnp
import numpy as np
from jax import lax
from jax.experimental import pallas as pl
from jax.experimental.pallas import tpu as pltpu
from jax.sharding import PartitionSpec as P

POLAR_ITERS = 12
Y_SIZE = 4
HALF = 128
BLOCKS = 24
CHUNK = 256
F32 = jnp.float32
BF16 = jnp.bfloat16
NT = (((1,), (1,)), ((), ()))
NN = (((1,), (0,)), ((), ()))
TN = (((0,), (0,)), ((), ()))


def pair_ring(count):
    return list(range(0, count, 2)) + list(range(count - 1, 0, -2))


def moved(top, bottom):
    count = len(top)
    new_top = [top[0], bottom[0]] + top[1 : count - 1]
    new_bottom = bottom[1:] + [top[count - 1]]
    return new_top, new_bottom


def routing(count):
    ring = pair_ring(count)
    place = {pair: at for at, pair in enumerate(ring)}
    top, bottom = [(c, 0) for c in range(count)], [(c, 1) for c in range(count)]
    top_1, bottom_1 = moved(top, bottom)
    ends = [{top_1[m][0]: (0, top_1[m][1]), bottom_1[m][0]: (1, bottom_1[m][1])} for m in range(count)]
    top_2, bottom_2 = moved([(m, 0) for m in range(count)], [(m, 1) for m in range(count)])
    rows = []
    for c in range(count):
        left, right = ring[place[c] - 1], ring[(place[c] + 1) % count]
        edge_l = next(m for m in range(count) if set(ends[m]) == {left, c})
        edge_r = next(m for m in range(count) if set(ends[m]) == {right, c})
        swap_2 = int(top_2[c][0] == edge_r)
        take_l, take_r = (bottom_2[c], top_2[c]) if swap_2 else (top_2[c], bottom_2[c])
        assert (take_l[0], take_r[0]) == (edge_l, edge_r)
        flip_l, flip_r = ends[edge_l][c][0] == 0, ends[edge_r][c][0] == 1
        rows.append([
            left, right, edge_l, edge_r,
            ends[edge_l][left][1], ends[edge_l][c][1], ends[edge_r][c][1], ends[edge_r][right][1],
            int(flip_l), int(flip_r),
            int(take_l[1] == ends[edge_l][c][0]), int(take_r[1] == ends[edge_r][right][0]),
            swap_2,
        ])
    return np.array(rows, np.int32)


def dot(left, right, dims):
    return lax.dot_general(left, right, dims, preferred_element_type=F32)


def split(value):
    high = value.astype(BF16)
    return high, (value - high.astype(F32)).astype(BF16)


def fine(left, right, dims):
    if left.dtype == BF16:
        high, low = split(right)
        return dot(left, high, dims) + dot(left, low, dims)
    high, low = split(left)
    return dot(high, right, dims) + dot(low, right, dims)


def gram_kernel(left_ref, own_ref, right_ref, out_ref):
    blocks = (left_ref, own_ref, right_ref)
    at = 0
    for i in range(3):
        for j in range(i, 3):
            gram = dot(blocks[i][...], blocks[j][...], TN).astype(BF16)
            for a in range(2):
                for b in range(2):
                    out_ref[at * HALF : (at + 1) * HALF, :] = gram[a * HALF : (a + 1) * HALF, b * HALF : (b + 1) * HALF]
                    at += 1


def polar_starts(grams, signs):
    order = 2 * HALF
    row = lax.broadcasted_iota(jnp.int32, (order, order), 0)
    column = lax.broadcasted_iota(jnp.int32, (order, order), 1)
    apart = (row < HALF) != (column < HALF)
    starts = []
    for gram, sign in zip(grams, signs):
        trace_mean = jnp.sum(jnp.where(row == column, gram, 0.0)) / order + 1e-06
        upper = jnp.where(row < column, gram, 0.0) / trace_mean
        upper = jnp.where(apart, sign * upper, upper)
        initial = jnp.where(row == column, 1.0, 0.5 * (upper - upper.T))
        starts.append(initial * lax.rsqrt(jnp.sum(initial * initial)))
    return starts


def refine(iterate):
    high, low = split(iterate)
    square = dot(high, high, NT) + dot(high, low, NT) + dot(low, high, NT)
    sq_high, sq_low = split(square)
    return 1.5 * iterate - 0.5 * (dot(high, sq_high, NN) + dot(high, sq_low, NN) + dot(low, sq_high, NN))


def polars(grams, signs):
    iterates = polar_starts(grams, signs)
    for _ in range(POLAR_ITERS):
        iterates = [refine(iterate) for iterate in iterates]
    return [iterate.astype(BF16) for iterate in iterates]


def half_of(value, which):
    return jnp.where(which == 1, value[:, HALF:], value[:, :HALF])


def joined(top_left, top_right, bottom_right):
    top = jnp.concatenate([top_left, top_right], axis=1)
    bottom = jnp.concatenate([top_right.T, bottom_right], axis=1)
    return jnp.concatenate([top, bottom], axis=0)


def rounds_kernel(total_rows, pair_ref, table_ref, orient_ref, gram_ref, left_ref, own_ref, right_ref, out_ref, rms_ref, turned, held):
    pair = pair_ref[0]
    look = lambda at: table_ref[pair, at]
    sign = lambda index, flip: (1 - 2 * (index ^ flip)).astype(F32)
    left, right, edge_l, edge_r = (look(at) for at in range(4))
    half_l, half_cl, half_cr, half_r, flip_l, flip_r, take_l, take_r, swap = (look(at) for at in range(4, 13))

    def block(at):
        part = lambda k: gram_ref[(4 * at + k) * HALF : (4 * at + k + 1) * HALF, :]
        top = jnp.concatenate([part(0), part(1)], axis=1)
        bottom = jnp.concatenate([part(2), part(3)], axis=1)
        return jnp.concatenate([top, bottom], axis=0)

    g_ll, g_lc, g_lr, g_cc, g_cr, g_rr = (block(at) for at in range(6))

    r_l, r_c, r_r = polars(
        [g_ll, g_cc, g_rr],
        [sign(orient_ref[at, 0], 0) for at in (left, pair, right)],
    )
    q_l, q_cl, q_cr, q_r = half_of(r_l, half_l), half_of(r_c, half_cl), half_of(r_c, half_cr), half_of(r_r, half_r)
    q_c = jnp.concatenate([q_cl, q_cr], axis=1)
    between = lambda a, g, b: fine(a, fine(g, b, NN), TN)
    gram_l = joined(between(q_l, g_ll, q_l), between(q_l, g_lc, q_cl), between(q_cl, g_cc, q_cl))
    gram_r = joined(between(q_cr, g_cc, q_cr), between(q_cr, g_cr, q_r), between(q_r, g_rr, q_r))
    cross = jnp.concatenate([
        jnp.concatenate([between(q_l, g_lc, q_cr), between(q_l, g_lr, q_r)], axis=1),
        jnp.concatenate([between(q_cl, g_cc, q_cr), between(q_cl, g_cr, q_r)], axis=1),
    ], axis=0)

    for at in range(0, held.shape[0], CHUNK):
        rows = slice(at, at + CHUNK)
        turned[rows, :HALF] = dot(left_ref[rows, :], q_l, NN).astype(BF16)
        turned[rows, HALF : 3 * HALF] = dot(own_ref[rows, :], q_c, NN).astype(BF16)
        turned[rows, 3 * HALF :] = dot(right_ref[rows, :], q_r, NN).astype(BF16)

    e_l, e_r = polars(
        [gram_l, gram_r],
        [sign(orient_ref[edge_l, 1], flip_l), sign(orient_ref[edge_r, 1], flip_r)],
    )
    v_l, v_r = half_of(e_l, take_l), half_of(e_r, take_r)
    gram = joined(between(v_l, gram_l, v_l), between(v_l, cross, v_r), between(v_r, gram_r, v_r))

    for at in range(0, held.shape[0], CHUNK):
        rows = slice(at, at + CHUNK)
        met_l = jnp.concatenate([turned[rows, :HALF], turned[rows, HALF : 2 * HALF]], axis=1)
        met_r = jnp.concatenate([turned[rows, 2 * HALF : 3 * HALF], turned[rows, 3 * HALF :]], axis=1)
        held[rows, :HALF] = dot(met_l, v_l, NN).astype(BF16)
        held[rows, HALF:] = dot(met_r, v_r, NN).astype(BF16)

    (turn,) = polars([gram], [sign(orient_ref[pair, 2], swap)])
    turn = jnp.where(swap == 1, jnp.concatenate([turn[:, HALF:], turn[:, :HALF]], axis=1), turn)
    for at in range(0, held.shape[0], CHUNK):
        rows = slice(at, at + CHUNK)
        out_ref[rows, :] = dot(held[rows, :], turn, NN).astype(BF16)
    squares = jnp.sum(turn.astype(F32) * fine(gram, turn, NN), axis=0, keepdims=True)
    rms_ref[...] = jnp.sqrt(jnp.maximum(squares, 0.0) / total_rows)


def per_device(snapshots, orient):
    rows_axis, pairs = lax.axis_size("rows"), lax.axis_size("cols")
    z_size = rows_axis // Y_SIZE
    along_y = [[z * Y_SIZE + y for y in range(Y_SIZE)] for z in range(z_size)]
    along_z = [[z * Y_SIZE + y for z in range(z_size)] for y in range(Y_SIZE)]
    ring = pair_ring(pairs)
    forward = [(ring[at - 1], ring[at]) for at in range(pairs)]
    backward = [(target, source) for source, target in forward]

    def swapped(value, groups):
        return lax.all_to_all(value, "rows", 0, 0, axis_index_groups=groups, tiled=True)

    with jax.named_scope("neighbours"):
        left = lax.ppermute(snapshots, "cols", forward)
        right = lax.ppermute(snapshots, "cols", backward)
        turns = jnp.broadcast_to(jnp.pad(orient.reshape(1, 1, 3), ((0, 0), (0, 0), (0, HALF - 3))), (pairs, 1, HALF))
        turns = lax.all_to_all(turns, "cols", 0, 0, tiled=True).reshape(pairs, HALF)
    with jax.named_scope("gram"):
        gram = pl.pallas_call(
            gram_kernel,
            out_shape=jax.ShapeDtypeStruct((BLOCKS * HALF, HALF), BF16),
            compiler_params=pltpu.CompilerParams(vmem_limit_bytes=48 << 20),
        )(left, snapshots, right)
    with jax.named_scope("gram_sum"):
        part = swapped(gram.reshape(Y_SIZE, -1, HALF), along_y)
        part = jnp.sum(part.astype(F32), axis=0).astype(BF16)
        part = swapped(part.reshape(z_size, -1, HALF), along_z)
        part = jnp.sum(part.astype(F32), axis=0)
        part = swapped(jnp.broadcast_to(part[None], (z_size, *part.shape)), along_z).reshape(-1, HALF)
        gram = swapped(jnp.broadcast_to(part[None], (Y_SIZE, *part.shape)), along_y).reshape(-1, HALF)
    with jax.named_scope("rounds"):
        smem, vmem = pl.BlockSpec(memory_space=pltpu.SMEM), pl.BlockSpec(memory_space=pltpu.VMEM)
        rotated, column_rms = pl.pallas_call(
            functools.partial(rounds_kernel, snapshots.shape[0] * rows_axis),
            out_shape=(jax.ShapeDtypeStruct(snapshots.shape, BF16), jax.ShapeDtypeStruct((1, 2 * HALF), F32)),
            in_specs=[smem, smem, smem, vmem, vmem, vmem, vmem],
            out_specs=(vmem, vmem),
            scratch_shapes=[pltpu.VMEM((snapshots.shape[0], 4 * HALF), BF16), pltpu.VMEM(snapshots.shape, BF16)],
            compiler_params=pltpu.CompilerParams(vmem_limit_bytes=48 << 20),
        )(lax.axis_index("cols").reshape(1), jnp.asarray(routing(pairs)), turns, gram, left, snapshots, right)
    return rotated, column_rms.reshape(-1)


def solution(mesh):
    in_specs = (P("rows", "cols"), P(None, "cols"))
    out_specs = (P("rows", "cols"), P("cols"))
    return jax.shard_map(
        per_device, mesh=mesh, in_specs=in_specs, out_specs=out_specs, check_vma=False
    )
```

```python
import functools

import jax
import jax.numpy as jnp
import numpy as np
from jax import lax
from jax.experimental import pallas as pl
from jax.experimental.pallas import tpu as pltpu
from jax.sharding import PartitionSpec as P

POLAR_ITERS = 12
Y_SIZE = 4
HALF = 128
CHUNK = 256
F32 = jnp.float32
BF16 = jnp.bfloat16
NT = (((1,), (1,)), ((), ()))
NN = (((1,), (0,)), ((), ()))
TN = (((0,), (0,)), ((), ()))


def pair_ring(count):
    return list(range(0, count, 2)) + list(range(count - 1, 0, -2))


def moved(top, bottom):
    count = len(top)
    new_top = [top[0], bottom[0]] + top[1 : count - 1]
    new_bottom = bottom[1:] + [top[count - 1]]
    return new_top, new_bottom


def routing(count):
    ring = pair_ring(count)
    place = {pair: at for at, pair in enumerate(ring)}
    top, bottom = [(c, 0) for c in range(count)], [(c, 1) for c in range(count)]
    top_1, bottom_1 = moved(top, bottom)
    ends = [{top_1[m][0]: (0, top_1[m][1]), bottom_1[m][0]: (1, bottom_1[m][1])} for m in range(count)]
    top_2, bottom_2 = moved([(m, 0) for m in range(count)], [(m, 1) for m in range(count)])
    rows = []
    for c in range(count):
        left, right = ring[place[c] - 1], ring[(place[c] + 1) % count]
        edge_l = next(m for m in range(count) if set(ends[m]) == {left, c})
        edge_r = next(m for m in range(count) if set(ends[m]) == {right, c})
        swap_2 = int(top_2[c][0] == edge_r)
        take_l, take_r = (bottom_2[c], top_2[c]) if swap_2 else (top_2[c], bottom_2[c])
        assert (take_l[0], take_r[0]) == (edge_l, edge_r)
        flip_l, flip_r = ends[edge_l][c][0] == 0, ends[edge_r][c][0] == 1
        rows.append([
            left, right, edge_l, edge_r,
            ends[edge_l][left][1], ends[edge_l][c][1], ends[edge_r][c][1], ends[edge_r][right][1],
            int(flip_l), int(flip_r),
            int(take_l[1] == ends[edge_l][c][0]), int(take_r[1] == ends[edge_r][right][0]),
            swap_2,
        ])
    return np.array(rows, np.int32)


def dot(left, right, dims):
    return lax.dot_general(left, right, dims, preferred_element_type=F32)


def split(value):
    high = value.astype(BF16)
    return high, (value - high.astype(F32)).astype(BF16)


def fine(left, right, dims):
    if left.dtype == BF16:
        high, low = split(right)
        return dot(left, high, dims) + dot(left, low, dims)
    high, low = split(left)
    return dot(high, right, dims) + dot(low, right, dims)


def triangle(shape):
    return lax.broadcasted_iota(jnp.int32, shape, 0), lax.broadcasted_iota(jnp.int32, shape, 1)


def own_gram_kernel(own_ref, out_ref):
    total = dot(own_ref[...], own_ref[...], TN)
    first, apart, second = total[:HALF, :HALF], total[:HALF, HALF:], total[HALF:, HALF:]
    row, column = triangle(first.shape)
    diagonal = jnp.sum(jnp.where(row == column, second, 0.0), axis=0, keepdims=True)
    packed = jnp.concatenate([jnp.where(row <= column, first, second), apart], axis=0)
    pieces, rows = out_ref.shape[0], out_ref.shape[1] - 8
    for at in range(pieces):
        out_ref[at, :rows] = packed[at * rows : (at + 1) * rows]
        out_ref[at, rows:] = jnp.broadcast_to(diagonal, (8, HALF))


def cross_gram_kernel(left_ref, own_ref, right_ref, gram_ref, out_ref):
    per_device, piece = 3 * HALF, gram_ref.shape[1] - 8
    total = jnp.sum(gram_ref[...], axis=0)
    high = total.astype(BF16).astype(F32)
    low = total - high
    extra = jnp.concatenate([high[:piece], low[:piece], high[piece:], low[piece:]], axis=0).astype(BF16)
    for at in range(out_ref.shape[0]):
        out_ref[at, per_device:] = extra
    pairs = (left_ref, own_ref), (own_ref, right_ref), (left_ref, right_ref)
    totals = [dot(one[...], two[...], TN) for one, two in pairs]
    for at in range(12):
        a, b, row = at // 2 % 2, at % 2, at % 3 * HALF
        block = totals[at // 4][a * HALF : (a + 1) * HALF, b * HALF : (b + 1) * HALF]
        out_ref[at // 3, row : row + HALF] = block.astype(BF16)


def summed_y_kernel(both_ref, out_ref, diagonal_ref):
    count, per_device = out_ref.shape[0], 3 * HALF
    step = per_device // count
    piece = out_ref.shape[1] - step
    cross = sum(both_ref[y, :per_device].astype(F32) for y in range(Y_SIZE))
    extra = sum(both_ref[y, per_device:].astype(F32) for y in range(Y_SIZE))
    gram = extra[:piece] + extra[piece : 2 * piece]
    diagonal_ref[...] = extra[2 * piece : 2 * piece + 8] + extra[2 * piece + 8 :]
    for at in range(count):
        out_ref[at, :step] = cross[at * step : (at + 1) * step]
        out_ref[at, step:] = gram


def summed_z_kernel(both_ref, out_ref, gram_ref):
    count, step = out_ref.shape[:2]
    piece = both_ref.shape[1] - step
    cross = jnp.sum(both_ref[:, :step], axis=0)
    for at in range(count):
        out_ref[at] = cross
        gram_ref[at * piece : (at + 1) * piece] = both_ref[at, step:]


def unpacked(packed_ref, diagonal):
    both, apart = packed_ref[:HALF, :], packed_ref[HALF:, :]
    row, column = triangle(both.shape)
    turned = both.T
    first = jnp.where(row <= column, both, turned)
    second = jnp.where(row == column, diagonal, jnp.where(row > column, both, turned))
    return joined(first, apart, second)


def block_of(part):
    top = jnp.concatenate([part(0), part(1)], axis=1)
    bottom = jnp.concatenate([part(2), part(3)], axis=1)
    return jnp.concatenate([top, bottom], axis=0)


def polar_starts(grams, signs):
    order = 2 * HALF
    row = lax.broadcasted_iota(jnp.int32, (order, order), 0)
    column = lax.broadcasted_iota(jnp.int32, (order, order), 1)
    apart = (row < HALF) != (column < HALF)
    starts = []
    for gram, sign in zip(grams, signs):
        trace_mean = jnp.sum(jnp.where(row == column, gram, 0.0)) / order + 1e-06
        upper = jnp.where(row < column, gram, 0.0) / trace_mean
        upper = jnp.where(apart, sign * upper, upper)
        initial = jnp.where(row == column, 1.0, 0.5 * (upper - upper.T))
        starts.append(initial * lax.rsqrt(jnp.sum(initial * initial)))
    return starts


def refine(iterate):
    high, low = split(iterate)
    square = dot(high, high, NT) + dot(high, low, NT) + dot(low, high, NT)
    sq_high, sq_low = split(square)
    return 1.5 * iterate - 0.5 * (dot(sq_high, high, NN) + dot(sq_low, high, NN) + dot(sq_high, low, NN))


def polars(grams, signs):
    iterates = polar_starts(grams, signs)
    for _ in range(POLAR_ITERS):
        iterates = [refine(iterate) for iterate in iterates]
    return [iterate.astype(BF16) for iterate in iterates]


def half_of(value, which):
    return jnp.where(which == 1, value[:, HALF:], value[:, :HALF])


def joined(top_left, top_right, bottom_right):
    top = jnp.concatenate([top_left, top_right], axis=1)
    bottom = jnp.concatenate([top_right.T, bottom_right], axis=1)
    return jnp.concatenate([top, bottom], axis=0)


def between(one, gram, two):
    return fine(one, fine(gram, two, NN), TN)


def sign_of(flag, flip):
    return (1 - 2 * (flag ^ flip)).astype(F32)


def first_round_kernel(pair_ref, table_ref, orient_ref, gram_ref, diagonal_ref, back_ref, ahead_ref, mid_ref):
    pair = pair_ref[0]
    gram = unpacked(gram_ref, diagonal_ref[:1, :])
    (turn,) = polars([gram], [sign_of(orient_ref[0], 0)])
    q_cl, q_cr = half_of(turn, table_ref[pair, 5]), half_of(turn, table_ref[pair, 6])
    for ref, q in ((back_ref, q_cl), (ahead_ref, q_cr)):
        high, low = split(between(q, gram, q))
        ref[: 2 * HALF, :] = q
        ref[2 * HALF : 3 * HALF, :] = high
        ref[3 * HALF :, :] = low
    mid_ref[...] = between(q_cl, gram, q_cr)


def rounds_kernel(
    total_rows, pair_ref, table_ref, orient_ref, below_ref, above_ref,
    *rest,
):
    sources, (out_ref, rms_ref), (*kept, held, arrived) = rest[:9], rest[9:11], rest[11:]
    copies = [pltpu.make_async_copy(source, place, arrived.at[at]) for at, (source, place) in enumerate(zip(sources, kept))]
    for copy in copies:
        copy.start()
    gram_ref, from_left_ref, back_ref, ahead_ref, from_right_ref, mid_ref, left_ref, own_ref, right_ref = kept
    pair = pair_ref[0]
    look = lambda at: table_ref[pair, at]
    edge_l, edge_r, flip_l, flip_r, take_l, take_r, swap = (look(at) for at in (2, 3, 8, 9, 10, 11, 12))
    of_edge = lambda edge: jnp.where(edge < pair, below_ref[1], jnp.where(edge > pair, above_ref[1], orient_ref[1]))

    for copy in copies[:6]:
        copy.wait()
    g_lc, g_cr, g_lr = (block_of(lambda k: gram_ref[(4 * at + k) * HALF : (4 * at + k + 1) * HALF, :]) for at in range(3))
    q_l, q_cl, q_cr, q_r = (ref[: 2 * HALF, :] for ref in (from_left_ref, back_ref, ahead_ref, from_right_ref))
    d_l, d_cl, d_cr, d_r = (
        ref[2 * HALF : 3 * HALF, :].astype(F32) + ref[3 * HALF :, :].astype(F32)
        for ref in (from_left_ref, back_ref, ahead_ref, from_right_ref)
    )
    gram_l = joined(d_l, between(q_l, g_lc, q_cl), d_cl)
    gram_r = joined(d_cr, between(q_cr, g_cr, q_r), d_r)
    cross = jnp.concatenate([
        jnp.concatenate([between(q_l, g_lc, q_cr), between(q_l, g_lr, q_r)], axis=1),
        jnp.concatenate([mid_ref[...], between(q_cl, g_cr, q_r)], axis=1),
    ], axis=0)

    e_l, e_r = polars([gram_l, gram_r], [sign_of(of_edge(edge_l), flip_l), sign_of(of_edge(edge_r), flip_r)])
    v_l, v_r = half_of(e_l, take_l), half_of(e_r, take_r)
    gram = joined(between(v_l, gram_l, v_l), between(v_l, cross, v_r), between(v_r, gram_r, v_r))

    for copy in copies[6:]:
        copy.wait()
    q_c = jnp.concatenate([q_cl, q_cr], axis=1)
    for at in range(0, held.shape[0], CHUNK):
        rows = slice(at, at + CHUNK)
        turned_l = dot(left_ref[rows, :], q_l, NN).astype(BF16)
        turned_c = dot(own_ref[rows, :], q_c, NN).astype(BF16)
        turned_r = dot(right_ref[rows, :], q_r, NN).astype(BF16)
        met_l = jnp.concatenate([turned_l, turned_c[:, :HALF]], axis=1)
        met_r = jnp.concatenate([turned_c[:, HALF:], turned_r], axis=1)
        held[rows, :HALF] = dot(met_l, v_l, NN).astype(BF16)
        held[rows, HALF:] = dot(met_r, v_r, NN).astype(BF16)

    (turn,) = polars([gram], [sign_of(orient_ref[2], swap)])
    turn = jnp.where(swap == 1, jnp.concatenate([turn[:, HALF:], turn[:, :HALF]], axis=1), turn)
    for at in range(0, held.shape[0], CHUNK):
        rows = slice(at, at + CHUNK)
        out_ref[rows, :] = dot(held[rows, :], turn, NN).astype(BF16)
    squares = jnp.sum(turn.astype(F32) * fine(gram, turn, NN), axis=0, keepdims=True)
    rms_ref[...] = jnp.sqrt(jnp.maximum(squares, 0.0) / total_rows)


def call(kernel, outs, spaces, operands, micros, scratch=(), megabytes=8):
    space = {"s": pltpu.SMEM, "v": pltpu.VMEM, "a": pl.ANY}
    return pl.pallas_call(
        kernel,
        out_shape=outs,
        in_specs=[pl.BlockSpec(memory_space=space[name]) for name in spaces],
        out_specs=jax.tree.map(lambda _: pl.BlockSpec(memory_space=pltpu.VMEM), outs),
        scratch_shapes=scratch,
        compiler_params=pltpu.CompilerParams(vmem_limit_bytes=megabytes << 20),
        cost_estimate=pl.CostEstimate(flops=micros * 10**9, bytes_accessed=0, transcendentals=0),
    )(*operands)


def per_device(snapshots, orient):
    rows_axis, pairs = lax.axis_size("rows"), lax.axis_size("cols")
    z_size = rows_axis // Y_SIZE
    along_y = [[z * Y_SIZE + y for y in range(Y_SIZE)] for z in range(z_size)]
    along_z = [[z * Y_SIZE + y for z in range(z_size)] for y in range(Y_SIZE)]
    ring = pair_ring(pairs)
    forward = [(ring[at - 1], ring[at]) for at in range(pairs)]
    backward = [(target, source) for source, target in forward]
    shape = jax.ShapeDtypeStruct
    height = snapshots.shape[0]
    pair = lax.axis_index("cols").reshape(1)
    table = jnp.asarray(routing(pairs))
    orient = orient.reshape(-1)

    def swapped(value, count, groups):
        return lax.all_to_all(value.reshape(count, -1, HALF), "rows", 0, 0, axis_index_groups=groups, tiled=True)

    def gathered(value, count, groups):
        return swapped(jnp.broadcast_to(value[None], (count, *value.shape)), count, groups).reshape(-1, HALF)

    with jax.named_scope("neighbours"):
        left = lax.ppermute(snapshots, "cols", forward)
        right = lax.ppermute(snapshots, "cols", backward)
    with jax.named_scope("own_gram"):
        piece, step = 2 * HALF // z_size, 3 * HALF // z_size
        gram = call(
            own_gram_kernel, shape((z_size, piece + 8, HALF), F32), "v", (snapshots,), 1
        )
        gram = swapped(gram, z_size, along_z)
    left, right, gram = lax.optimization_barrier((left, right, gram))
    with jax.named_scope("sum_y"):
        both = call(
            cross_gram_kernel, shape((Y_SIZE, 3 * HALF + 2 * (piece + 8), HALF), BF16), "vvvv",
            (left, snapshots, right, gram), 2,
        )
        both = swapped(both, Y_SIZE, along_y)
        both, diagonal = call(
            summed_y_kernel, (shape((z_size, step + piece, HALF), F32), shape((8, HALF), F32)), "v", (both,), 1
        )
    both, orient = lax.optimization_barrier((both, orient))
    with jax.named_scope("neighbours"):
        below = lax.ppermute(orient, "cols", [(c - 1, c) for c in range(1, pairs)])
        above = lax.ppermute(orient, "cols", [(c, c - 1) for c in range(1, pairs)])
    with jax.named_scope("sum_z"):
        both = swapped(both, z_size, along_z)
        cross, gram = call(
            summed_z_kernel, (shape((z_size, step, HALF), F32), shape((2 * HALF, HALF), F32)), "v", (both,), 1
        )
    cross, gram, below, above = lax.optimization_barrier((cross, gram, below, above))
    with jax.named_scope("gather_z"):
        cross = swapped(cross, z_size, along_z).reshape(-1, HALF)
    with jax.named_scope("first_round"):
        sent = shape((4 * HALF, HALF), BF16)
        back, ahead, mid = call(
            first_round_kernel, (sent, sent, shape((HALF, HALF), F32)), "sssvv",
            (pair, table, orient, gram, diagonal), 9,
        )
    cross, back, ahead, mid = lax.optimization_barrier((cross, back, ahead, mid))
    with jax.named_scope("gather_y"):
        cross = gathered(cross, Y_SIZE, along_y)
    with jax.named_scope("neighbours"):
        from_left = lax.ppermute(ahead, "cols", forward)
        from_right = lax.ppermute(back, "cols", backward)
    with jax.named_scope("rounds"):
        operands = (cross, from_left, back, ahead, from_right, mid, left, snapshots, right)
        rotated, column_rms = call(
            functools.partial(rounds_kernel, height * rows_axis),
            (shape(snapshots.shape, BF16), shape((1, 2 * HALF), F32)),
            "sssss" + "a" * len(operands),
            (pair, table, orient, below, above, *operands),
            21,
            [pltpu.VMEM(value.shape, value.dtype) for value in operands]
            + [pltpu.VMEM(snapshots.shape, BF16), pltpu.SemaphoreType.DMA((len(operands),))],
            megabytes=52,
        )
    return rotated, column_rms.reshape(-1)


def solution(mesh):
    in_specs = (P("rows", "cols"), P(None, "cols"))
    out_specs = (P("rows", "cols"), P("cols"))
    return jax.shard_map(
        per_device, mesh=mesh, in_specs=in_specs, out_specs=out_specs, check_vma=False
    )
```

```python
import functools

import jax
import jax.numpy as jnp
import numpy as np
from jax import lax
from jax.experimental import pallas as pl
from jax.experimental.pallas import tpu as pltpu
from jax.sharding import PartitionSpec as P

POLAR_ITERS = 12
Y_SIZE = 4
HALF = 128
QUARTER = 2 * HALF // Y_SIZE
CHUNK = 256
F32 = jnp.float32
BF16 = jnp.bfloat16
NT = (((1,), (1,)), ((), ()))
NN = (((1,), (0,)), ((), ()))
TN = (((0,), (0,)), ((), ()))


def pair_ring(count):
    return list(range(0, count, 2)) + list(range(count - 1, 0, -2))


def moved(top, bottom):
    count = len(top)
    new_top = [top[0], bottom[0]] + top[1 : count - 1]
    new_bottom = bottom[1:] + [top[count - 1]]
    return new_top, new_bottom


def routing(count):
    ring = pair_ring(count)
    place = {pair: at for at, pair in enumerate(ring)}
    top, bottom = [(c, 0) for c in range(count)], [(c, 1) for c in range(count)]
    top_1, bottom_1 = moved(top, bottom)
    ends = [{top_1[m][0]: (0, top_1[m][1]), bottom_1[m][0]: (1, bottom_1[m][1])} for m in range(count)]
    top_2, bottom_2 = moved([(m, 0) for m in range(count)], [(m, 1) for m in range(count)])
    rows = []
    for c in range(count):
        left, right = ring[place[c] - 1], ring[(place[c] + 1) % count]
        edge_l = next(m for m in range(count) if set(ends[m]) == {left, c})
        edge_r = next(m for m in range(count) if set(ends[m]) == {right, c})
        swap_2 = int(top_2[c][0] == edge_r)
        take_l, take_r = (bottom_2[c], top_2[c]) if swap_2 else (top_2[c], bottom_2[c])
        assert (take_l[0], take_r[0]) == (edge_l, edge_r)
        flip_l, flip_r = ends[edge_l][c][0] == 0, ends[edge_r][c][0] == 1
        rows.append([
            left, right, edge_l, edge_r,
            ends[edge_l][left][1], ends[edge_l][c][1], ends[edge_r][c][1], ends[edge_r][right][1],
            int(flip_l), int(flip_r),
            int(take_l[1] == ends[edge_l][c][0]), int(take_r[1] == ends[edge_r][right][0]),
            swap_2,
        ])
    return np.array(rows, np.int32)


def dot(left, right, dims):
    return lax.dot_general(left, right, dims, preferred_element_type=F32)


def split(value):
    high = value.astype(BF16)
    return high, (value - high.astype(F32)).astype(BF16)


def fine(left, right, dims):
    if left.dtype == BF16:
        high, low = split(right)
        return dot(left, high, dims) + dot(left, low, dims)
    high, low = split(left)
    return dot(high, right, dims) + dot(low, right, dims)


def triangle(shape):
    return lax.broadcasted_iota(jnp.int32, shape, 0), lax.broadcasted_iota(jnp.int32, shape, 1)


def own_gram_kernel(own_ref, out_ref):
    total = dot(own_ref[...], own_ref[...], TN)
    first, apart, second = total[:HALF, :HALF], total[:HALF, HALF:], total[HALF:, HALF:]
    row, column = triangle(first.shape)
    diagonal = jnp.sum(jnp.where(row == column, second, 0.0), axis=0, keepdims=True)
    packed = jnp.concatenate([jnp.where(row <= column, first, second), apart], axis=0)
    pieces, rows = out_ref.shape[0], out_ref.shape[1] - 8
    for at in range(pieces):
        out_ref[at, :rows] = packed[at * rows : (at + 1) * rows]
        out_ref[at, rows:] = jnp.broadcast_to(diagonal, (8, HALF))


def cross_gram_kernel(left_ref, own_ref, right_ref, gram_ref, out_ref):
    per_device, piece = 3 * HALF, gram_ref.shape[1] - 8
    total = jnp.sum(gram_ref[...], axis=0)
    high = total.astype(BF16).astype(F32)
    low = total - high
    extra = jnp.concatenate([high[:piece], low[:piece], high[piece:], low[piece:]], axis=0).astype(BF16)
    for at in range(out_ref.shape[0]):
        out_ref[at, per_device:] = extra
    pairs = (own_ref, left_ref), (own_ref, right_ref), (left_ref, right_ref)
    for at, (one, two) in enumerate(pairs):
        gram = dot(one[...], two[...], TN).astype(BF16)
        for y in range(out_ref.shape[0]):
            for half in range(2):
                row = at * HALF + half * QUARTER
                out_ref[y, row : row + QUARTER] = gram[y * QUARTER : (y + 1) * QUARTER, half * HALF : (half + 1) * HALF]


def summed_y_kernel(both_ref, out_ref, diagonal_ref):
    count, per_device = out_ref.shape[0], 3 * HALF
    step = per_device // count
    piece = out_ref.shape[1] - step
    cross = sum(both_ref[y, :per_device].astype(F32) for y in range(Y_SIZE))
    extra = sum(both_ref[y, per_device:].astype(F32) for y in range(Y_SIZE))
    gram = extra[:piece] + extra[piece : 2 * piece]
    diagonal_ref[...] = extra[2 * piece : 2 * piece + 8] + extra[2 * piece + 8 :]
    for at in range(count):
        out_ref[at, :step] = cross[at * step : (at + 1) * step]
        out_ref[at, step:] = gram


def summed_z_kernel(both_ref, out_ref, gram_ref):
    count, step = out_ref.shape[:2]
    piece = both_ref.shape[1] - step
    cross = jnp.sum(both_ref[:, :step], axis=0)
    for at in range(count):
        out_ref[at] = cross
        gram_ref[at * piece : (at + 1) * piece] = both_ref[at, step:]


def unpacked(packed_ref, diagonal):
    both, apart = packed_ref[:HALF, :], packed_ref[HALF:, :]
    row, column = triangle(both.shape)
    turned = both.T
    first = jnp.where(row <= column, both, turned)
    second = jnp.where(row == column, diagonal, jnp.where(row > column, both, turned))
    return joined(first, apart, second)


def half_turned_kernel(cross_ref, from_left_ref, from_right_ref, out_ref):
    for at, q_ref in enumerate((from_left_ref, from_right_ref, from_right_ref)):
        row = at * HALF
        gram = jnp.concatenate([cross_ref[row : row + QUARTER, :], cross_ref[row + QUARTER : row + HALF, :]], axis=1)
        value = fine(gram, q_ref[: 2 * HALF, :], NN)
        for y in range(out_ref.shape[0]):
            out_ref[y, at * QUARTER : (at + 1) * QUARTER] = value


def polar_starts(grams, signs):
    order = 2 * HALF
    row, column = triangle((order, order))
    apart = (row < HALF) != (column < HALF)
    starts = []
    for gram, sign in zip(grams, signs):
        trace_mean = jnp.sum(jnp.where(row == column, gram, 0.0)) / order + 1e-06
        upper = jnp.where(row < column, gram, 0.0) / trace_mean
        upper = jnp.where(apart, sign * upper, upper)
        starts.append(jnp.where(row == column, 1.0, 0.5 * (upper - upper.T)))
    return starts


def cubed(iterate):
    high, low = split(iterate)
    square = dot(high, high, NT) + dot(high, low, NT) + dot(low, high, NT)
    sq_high, sq_low = split(square)
    return dot(sq_high, high, NN) + dot(sq_low, high, NN) + dot(sq_high, low, NN)


def first_step(start):
    inverse = lax.rsqrt(jnp.sum(start * start))
    return inverse * (1.5 * start - (0.5 * inverse * inverse) * cubed(start))


def polars(grams, signs):
    iterates = [first_step(start) for start in polar_starts(grams, signs)]
    for _ in range(POLAR_ITERS - 1):
        iterates = [1.5 * iterate - 0.5 * cubed(iterate) for iterate in iterates]
    return [iterate.astype(BF16) for iterate in iterates]


def half_of(value, which):
    return jnp.where(which == 1, value[:, HALF:], value[:, :HALF])


def joined(top_left, top_right, bottom_right):
    top = jnp.concatenate([top_left, top_right], axis=1)
    bottom = jnp.concatenate([top_right.T, bottom_right], axis=1)
    return jnp.concatenate([top, bottom], axis=0)


def between(one, gram, two):
    return fine(one, fine(gram, two, NN), TN)


def sign_of(flag, flip):
    return (1 - 2 * (flag ^ flip)).astype(F32)


def first_round_kernel(pair_ref, table_ref, orient_ref, gram_ref, diagonal_ref, back_ref, ahead_ref, mid_ref):
    pair = pair_ref[0]
    gram = unpacked(gram_ref, diagonal_ref[:1, :])
    (turn,) = polars([gram], [sign_of(orient_ref[0], 0)])
    q_cl, q_cr = half_of(turn, table_ref[pair, 5]), half_of(turn, table_ref[pair, 6])
    for ref, q in ((back_ref, q_cl), (ahead_ref, q_cr)):
        high, low = split(between(q, gram, q))
        ref[: 2 * HALF, :] = q
        ref[2 * HALF : 3 * HALF, :] = high
        ref[3 * HALF :, :] = low
    mid_ref[...] = between(q_cl, gram, q_cr)


def rounds_kernel(
    total_rows, pair_ref, table_ref, orient_ref, below_ref, above_ref,
    *rest,
):
    sources, (out_ref, rms_ref), (*kept, held, arrived) = rest[:9], rest[9:11], rest[11:]
    copies = [pltpu.make_async_copy(source, place, arrived.at[at]) for at, (source, place) in enumerate(zip(sources, kept))]
    for copy in copies[:6]:
        copy.start()
    gram_ref, from_left_ref, back_ref, ahead_ref, from_right_ref, mid_ref, left_ref, own_ref, right_ref = kept
    pair = pair_ref[0]
    look = lambda at: table_ref[pair, at]
    edge_l, edge_r, flip_l, flip_r, take_l, take_r, swap = (look(at) for at in (2, 3, 8, 9, 10, 11, 12))
    of_edge = lambda edge: jnp.where(edge < pair, below_ref[1], jnp.where(edge > pair, above_ref[1], orient_ref[1]))

    for copy in copies[:6]:
        copy.wait()
    for copy in copies[6:]:
        copy.start()
    c_l, c_r, l_r = (
        jnp.concatenate([gram_ref[y, at * QUARTER : (at + 1) * QUARTER] for y in range(Y_SIZE)], axis=0) for at in range(3)
    )
    q_l, q_cl, q_cr, q_r = (ref[: 2 * HALF, :] for ref in (from_left_ref, back_ref, ahead_ref, from_right_ref))
    d_l, d_cl, d_cr, d_r = (
        ref[2 * HALF : 3 * HALF, :].astype(F32) + ref[3 * HALF :, :].astype(F32)
        for ref in (from_left_ref, back_ref, ahead_ref, from_right_ref)
    )
    gram_l = joined(d_l, fine(q_cl, c_l, TN).T, d_cl)
    gram_r = joined(d_cr, fine(q_cr, c_r, TN), d_r)
    cross = jnp.concatenate([
        jnp.concatenate([fine(q_cr, c_l, TN).T, fine(q_l, l_r, TN)], axis=1),
        jnp.concatenate([mid_ref[...], fine(q_cl, c_r, TN)], axis=1),
    ], axis=0)

    e_l, e_r = polars([gram_l, gram_r], [sign_of(of_edge(edge_l), flip_l), sign_of(of_edge(edge_r), flip_r)])
    v_l, v_r = half_of(e_l, take_l), half_of(e_r, take_r)
    gram = joined(between(v_l, gram_l, v_l), between(v_l, cross, v_r), between(v_r, gram_r, v_r))

    for copy in copies[6:]:
        copy.wait()
    q_c = jnp.concatenate([q_cl, q_cr], axis=1)
    for at in range(0, held.shape[0], CHUNK):
        rows = slice(at, at + CHUNK)
        turned_l = dot(left_ref[rows, :], q_l, NN).astype(BF16)
        turned_c = dot(own_ref[rows, :], q_c, NN).astype(BF16)
        turned_r = dot(right_ref[rows, :], q_r, NN).astype(BF16)
        met_l = jnp.concatenate([turned_l, turned_c[:, :HALF]], axis=1)
        met_r = jnp.concatenate([turned_c[:, HALF:], turned_r], axis=1)
        held[rows, :HALF] = dot(met_l, v_l, NN).astype(BF16)
        held[rows, HALF:] = dot(met_r, v_r, NN).astype(BF16)

    (turn,) = polars([gram], [sign_of(orient_ref[2], swap)])
    turn = jnp.where(swap == 1, jnp.concatenate([turn[:, HALF:], turn[:, :HALF]], axis=1), turn)
    for at in range(0, held.shape[0], CHUNK):
        rows = slice(at, at + CHUNK)
        out_ref[rows, :] = dot(held[rows, :], turn, NN).astype(BF16)
    squares = jnp.sum(turn.astype(F32) * fine(gram, turn, NN), axis=0, keepdims=True)
    rms_ref[...] = jnp.sqrt(jnp.maximum(squares, 0.0) / total_rows)


def call(kernel, outs, spaces, operands, micros, scratch=(), megabytes=8):
    space = {"s": pltpu.SMEM, "v": pltpu.VMEM, "a": pl.ANY}
    return pl.pallas_call(
        kernel,
        out_shape=outs,
        in_specs=[pl.BlockSpec(memory_space=space[name]) for name in spaces],
        out_specs=jax.tree.map(lambda _: pl.BlockSpec(memory_space=pltpu.VMEM), outs),
        scratch_shapes=scratch,
        compiler_params=pltpu.CompilerParams(vmem_limit_bytes=megabytes << 20),
        cost_estimate=pl.CostEstimate(flops=micros * 10**9, bytes_accessed=0, transcendentals=0),
    )(*operands)


def per_device(snapshots, orient):
    rows_axis, pairs = lax.axis_size("rows"), lax.axis_size("cols")
    z_size = rows_axis // Y_SIZE
    along_y = [[z * Y_SIZE + y for y in range(Y_SIZE)] for z in range(z_size)]
    along_z = [[z * Y_SIZE + y for z in range(z_size)] for y in range(Y_SIZE)]
    ring = pair_ring(pairs)
    forward = [(ring[at - 1], ring[at]) for at in range(pairs)]
    backward = [(target, source) for source, target in forward]
    shape = jax.ShapeDtypeStruct
    height = snapshots.shape[0]
    pair = lax.axis_index("cols").reshape(1)
    table = jnp.asarray(routing(pairs))
    orient = orient.reshape(-1)

    def swapped(value, count, groups):
        return lax.all_to_all(value.reshape(count, -1, HALF), "rows", 0, 0, axis_index_groups=groups, tiled=True)

    with jax.named_scope("neighbours"):
        left = lax.ppermute(snapshots, "cols", forward)
        right = lax.ppermute(snapshots, "cols", backward)
    with jax.named_scope("own_gram"):
        piece, step = 2 * HALF // z_size, 3 * HALF // z_size
        gram = call(
            own_gram_kernel, shape((z_size, piece + 8, HALF), F32), "v", (snapshots,), 1
        )
        gram = swapped(gram, z_size, along_z)
    left, right, gram = lax.optimization_barrier((left, right, gram))
    with jax.named_scope("sum_y"):
        both = call(
            cross_gram_kernel, shape((Y_SIZE, 3 * HALF + 2 * (piece + 8), HALF), BF16), "vvvv",
            (left, snapshots, right, gram), 2,
        )
        both = swapped(both, Y_SIZE, along_y)
        both, diagonal = call(
            summed_y_kernel, (shape((z_size, step + piece, HALF), F32), shape((8, HALF), F32)), "v", (both,), 1
        )
    both, orient = lax.optimization_barrier((both, orient))
    with jax.named_scope("neighbours"):
        below = lax.ppermute(orient, "cols", [(c - 1, c) for c in range(1, pairs)])
        above = lax.ppermute(orient, "cols", [(c, c - 1) for c in range(1, pairs)])
    with jax.named_scope("sum_z"):
        both = swapped(both, z_size, along_z)
        cross, gram = call(
            summed_z_kernel, (shape((z_size, step, HALF), F32), shape((2 * HALF, HALF), F32)), "v", (both,), 1
        )
    cross, gram, below, above = lax.optimization_barrier((cross, gram, below, above))
    with jax.named_scope("gather_z"):
        cross = swapped(cross, z_size, along_z).reshape(-1, HALF)
    with jax.named_scope("first_round"):
        sent = shape((4 * HALF, HALF), BF16)
        back, ahead, mid = call(
            first_round_kernel, (sent, sent, shape((HALF, HALF), F32)), "sssvv",
            (pair, table, orient, gram, diagonal), 9,
        )
    with jax.named_scope("neighbours"):
        from_left = lax.ppermute(ahead, "cols", forward)
        from_right = lax.ppermute(back, "cols", backward)
    cross, from_left, from_right = lax.optimization_barrier((cross, from_left, from_right))
    with jax.named_scope("gather_y"):
        cross = call(
            half_turned_kernel, shape((Y_SIZE, 3 * QUARTER, HALF), F32), "vvv", (cross, from_left, from_right), 1
        )
        cross = swapped(cross, Y_SIZE, along_y)
    with jax.named_scope("rounds"):
        operands = (cross, from_left, back, ahead, from_right, mid, left, snapshots, right)
        rotated, column_rms = call(
            functools.partial(rounds_kernel, height * rows_axis),
            (shape(snapshots.shape, BF16), shape((1, 2 * HALF), F32)),
            "sssss" + "a" * len(operands),
            (pair, table, orient, below, above, *operands),
            21,
            [pltpu.VMEM(value.shape, value.dtype) for value in operands]
            + [pltpu.VMEM(snapshots.shape, BF16), pltpu.SemaphoreType.DMA((len(operands),))],
            megabytes=52,
        )
    return rotated, column_rms.reshape(-1)


def solution(mesh):
    in_specs = (P("rows", "cols"), P(None, "cols"))
    out_specs = (P("rows", "cols"), P("cols"))
    return jax.shard_map(
        per_device, mesh=mesh, in_specs=in_specs, out_specs=out_specs, check_vma=False
    )
```

```python
import functools

import jax
import jax.numpy as jnp
import numpy as np
from jax import lax
from jax.experimental import pallas as pl
from jax.experimental.pallas import tpu as pltpu
from jax.sharding import PartitionSpec as P

POLAR_ITERS = 12
Y_SIZE = 4
HALF = 128
QUARTER = 2 * HALF // Y_SIZE
CHUNK = 512
F32 = jnp.float32
BF16 = jnp.bfloat16
NT = (((1,), (1,)), ((), ()))
NN = (((1,), (0,)), ((), ()))
TN = (((0,), (0,)), ((), ()))


def pair_ring(count):
    return list(range(0, count, 2)) + list(range(count - 1, 0, -2))


def moved(top, bottom):
    count = len(top)
    new_top = [top[0], bottom[0]] + top[1 : count - 1]
    new_bottom = bottom[1:] + [top[count - 1]]
    return new_top, new_bottom


def routing(count):
    ring = pair_ring(count)
    place = {pair: at for at, pair in enumerate(ring)}
    top, bottom = [(c, 0) for c in range(count)], [(c, 1) for c in range(count)]
    top_1, bottom_1 = moved(top, bottom)
    ends = [{top_1[m][0]: (0, top_1[m][1]), bottom_1[m][0]: (1, bottom_1[m][1])} for m in range(count)]
    top_2, bottom_2 = moved([(m, 0) for m in range(count)], [(m, 1) for m in range(count)])
    rows = []
    for c in range(count):
        left, right = ring[place[c] - 1], ring[(place[c] + 1) % count]
        edge_l = next(m for m in range(count) if set(ends[m]) == {left, c})
        edge_r = next(m for m in range(count) if set(ends[m]) == {right, c})
        swap_2 = int(top_2[c][0] == edge_r)
        take_l, take_r = (bottom_2[c], top_2[c]) if swap_2 else (top_2[c], bottom_2[c])
        assert (take_l[0], take_r[0]) == (edge_l, edge_r)
        flip_l, flip_r = ends[edge_l][c][0] == 0, ends[edge_r][c][0] == 1
        rows.append([
            left, right, edge_l, edge_r,
            ends[edge_l][left][1], ends[edge_l][c][1], ends[edge_r][c][1], ends[edge_r][right][1],
            int(flip_l), int(flip_r),
            int(take_l[1] == ends[edge_l][c][0]), int(take_r[1] == ends[edge_r][right][0]),
            swap_2,
        ])
    return np.array(rows, np.int32)


def dot(left, right, dims):
    return lax.dot_general(left, right, dims, preferred_element_type=F32)


def split(value):
    high = value.astype(BF16)
    return high, (value - high.astype(F32)).astype(BF16)


def fine(left, right, dims):
    if left.dtype == BF16:
        high, low = split(right)
        return dot(left, high, dims) + dot(left, low, dims)
    high, low = split(left)
    return dot(high, right, dims) + dot(low, right, dims)


def triangle(shape):
    return lax.broadcasted_iota(jnp.int32, shape, 0), lax.broadcasted_iota(jnp.int32, shape, 1)


def own_gram_kernel(own_ref, out_ref):
    total = dot(own_ref[...], own_ref[...], TN)
    first, apart, second = total[:HALF, :HALF], total[:HALF, HALF:], total[HALF:, HALF:]
    row, column = triangle(first.shape)
    diagonal = jnp.sum(jnp.where(row == column, second, 0.0), axis=0, keepdims=True)
    packed = jnp.concatenate([jnp.where(row <= column, first, second), apart], axis=0)
    pieces, rows = out_ref.shape[0], out_ref.shape[1] - 8
    for at in range(pieces):
        out_ref[at, :rows] = packed[at * rows : (at + 1) * rows]
        out_ref[at, rows:] = jnp.broadcast_to(diagonal, (8, HALF))


def cross_gram_kernel(left_ref, own_ref, right_ref, gram_ref, out_ref):
    per_device, piece = 3 * HALF, gram_ref.shape[1] - 8
    total = jnp.sum(gram_ref[...], axis=0)
    high = total.astype(BF16).astype(F32)
    low = total - high
    extra = jnp.concatenate([high[:piece], low[:piece], high[piece:], low[piece:]], axis=0).astype(BF16)
    for at in range(out_ref.shape[0]):
        out_ref[at, per_device:] = extra
    pairs = (own_ref, left_ref), (own_ref, right_ref), (left_ref, right_ref)
    for at, (one, two) in enumerate(pairs):
        gram = dot(one[...], two[...], TN).astype(BF16)
        for y in range(out_ref.shape[0]):
            for half in range(2):
                row = at * HALF + half * QUARTER
                out_ref[y, row : row + QUARTER] = gram[y * QUARTER : (y + 1) * QUARTER, half * HALF : (half + 1) * HALF]


def summed_y_kernel(both_ref, out_ref, diagonal_ref):
    count, per_device = out_ref.shape[0], 3 * HALF
    step = per_device // count
    piece = out_ref.shape[1] - step
    cross = sum(both_ref[y, :per_device].astype(F32) for y in range(Y_SIZE))
    extra = sum(both_ref[y, per_device:].astype(F32) for y in range(Y_SIZE))
    gram = extra[:piece] + extra[piece : 2 * piece]
    diagonal_ref[...] = extra[2 * piece : 2 * piece + 8] + extra[2 * piece + 8 :]
    for at in range(count):
        out_ref[at, :step] = cross[at * step : (at + 1) * step]
        out_ref[at, step:] = gram


def summed_z_kernel(both_ref, out_ref, gram_ref):
    count, step = out_ref.shape[:2]
    piece = both_ref.shape[1] - step
    cross = jnp.sum(both_ref[:, :step], axis=0)
    for at in range(count):
        out_ref[at] = cross
        gram_ref[at * piece : (at + 1) * piece] = both_ref[at, step:]


def unpacked(packed_ref, diagonal):
    both, apart = packed_ref[:HALF, :], packed_ref[HALF:, :]
    row, column = triangle(both.shape)
    turned = both.T
    first = jnp.where(row <= column, both, turned)
    second = jnp.where(row == column, diagonal, jnp.where(row > column, both, turned))
    return joined(first, apart, second)


def half_turned_kernel(cross_ref, from_left_ref, from_right_ref, out_ref):
    for at, q_ref in enumerate((from_left_ref, from_right_ref, from_right_ref)):
        row = at * HALF
        gram = jnp.concatenate([cross_ref[row : row + QUARTER, :], cross_ref[row + QUARTER : row + HALF, :]], axis=1)
        value = fine(gram, q_ref[: 2 * HALF, :], NN)
        for y in range(out_ref.shape[0]):
            out_ref[y, at * QUARTER : (at + 1) * QUARTER] = value


def polar_starts(grams, signs):
    order = 2 * HALF
    row, column = triangle((order, order))
    apart = (row < HALF) != (column < HALF)
    starts = []
    for gram, sign in zip(grams, signs):
        trace_mean = jnp.sum(jnp.where(row == column, gram, 0.0)) / order + 1e-06
        upper = jnp.where(row < column, gram, 0.0) / trace_mean
        upper = jnp.where(apart, sign * upper, upper)
        starts.append(jnp.where(row == column, 1.0, 0.5 * (upper - upper.T)))
    return starts


def cubed(iterate):
    high, low = split(iterate)
    square = dot(high, high, NT) + dot(high, low, NT) + dot(low, high, NT)
    sq_high, sq_low = split(square)
    return dot(sq_high, high, NN) + dot(sq_low, high, NN) + dot(sq_high, low, NN)


def first_step(start):
    inverse = lax.rsqrt(jnp.sum(start * start))
    return inverse * (1.5 * start - (0.5 * inverse * inverse) * cubed(start))


def polars(grams, signs):
    iterates = [first_step(start) for start in polar_starts(grams, signs)]
    for _ in range(POLAR_ITERS - 1):
        iterates = [1.5 * iterate - 0.5 * cubed(iterate) for iterate in iterates]
    return [iterate.astype(BF16) for iterate in iterates]


def half_of(value, which):
    return jnp.where(which == 1, value[:, HALF:], value[:, :HALF])


def joined(top_left, top_right, bottom_right):
    top = jnp.concatenate([top_left, top_right], axis=1)
    bottom = jnp.concatenate([top_right.T, bottom_right], axis=1)
    return jnp.concatenate([top, bottom], axis=0)


def sign_of(flag, flip):
    return (1 - 2 * (flag ^ flip)).astype(F32)


def first_round_kernel(pair_ref, table_ref, orient_ref, gram_ref, diagonal_ref, back_ref, ahead_ref, mid_ref):
    pair = pair_ref[0]
    gram = unpacked(gram_ref, diagonal_ref[:1, :])
    (turn,) = polars([gram], [sign_of(orient_ref[0], 0)])
    q_c = jnp.concatenate([half_of(turn, table_ref[pair, 5]), half_of(turn, table_ref[pair, 6])], axis=1)
    after = fine(q_c, fine(gram, q_c, NN), TN)
    for ref, half in ((back_ref, slice(0, HALF)), (ahead_ref, slice(HALF, 2 * HALF))):
        high, low = split(after[half, half])
        ref[: 2 * HALF, :] = q_c[:, half]
        ref[2 * HALF : 3 * HALF, :] = high
        ref[3 * HALF :, :] = low
    mid_ref[...] = after[:HALF, HALF:]


def rounds_kernel(
    total_rows, pair_ref, table_ref, orient_ref, below_ref, above_ref,
    *rest,
):
    sources, (out_ref, rms_ref), (*kept, held, arrived) = rest[:9], rest[9:11], rest[11:]
    copies = [pltpu.make_async_copy(source, place, arrived.at[at]) for at, (source, place) in enumerate(zip(sources, kept))]
    for copy in copies[:6]:
        copy.start()
    gram_ref, from_left_ref, back_ref, ahead_ref, from_right_ref, mid_ref, left_ref, own_ref, right_ref = kept
    pair = pair_ref[0]
    look = lambda at: table_ref[pair, at]
    edge_l, edge_r, flip_l, flip_r, take_l, take_r, swap = (look(at) for at in (2, 3, 8, 9, 10, 11, 12))
    of_edge = lambda edge: jnp.where(edge < pair, below_ref[1], jnp.where(edge > pair, above_ref[1], orient_ref[1]))

    for copy in copies[:6]:
        copy.wait()
    for copy in copies[6:]:
        copy.start()
    c_l, c_r, l_r = (
        jnp.concatenate([gram_ref[y, at * QUARTER : (at + 1) * QUARTER] for y in range(Y_SIZE)], axis=0) for at in range(3)
    )
    q_l, q_cl, q_cr, q_r = (ref[: 2 * HALF, :] for ref in (from_left_ref, back_ref, ahead_ref, from_right_ref))
    d_l, d_cl, d_cr, d_r = (
        ref[2 * HALF : 3 * HALF, :].astype(F32) + ref[3 * HALF :, :].astype(F32)
        for ref in (from_left_ref, back_ref, ahead_ref, from_right_ref)
    )
    q_c = jnp.concatenate([q_cl, q_cr], axis=1)
    met = fine(q_c, jnp.concatenate([c_l, c_r], axis=1), TN)
    gram_l = joined(d_l, met[:HALF, :HALF].T, d_cl)
    gram_r = joined(d_cr, met[HALF:, HALF:], d_r)
    cross = jnp.concatenate([
        jnp.concatenate([met[HALF:, :HALF].T, fine(q_l, l_r, TN)], axis=1),
        jnp.concatenate([mid_ref[...], met[:HALF, HALF:]], axis=1),
    ], axis=0)

    e_l, e_r = polars([gram_l, gram_r], [sign_of(of_edge(edge_l), flip_l), sign_of(of_edge(edge_r), flip_r)])
    v_l, v_r = half_of(e_l, take_l), half_of(e_r, take_r)
    by_l = fine(gram_l, v_l, NN)
    by_r = fine(jnp.concatenate([cross, gram_r], axis=0), v_r, NN)
    top = fine(v_l, jnp.concatenate([by_l, by_r[: 2 * HALF]], axis=1), TN)
    gram = joined(top[:, :HALF], top[:, HALF:], fine(v_r, by_r[2 * HALF :], TN))

    for copy in copies[6:]:
        copy.wait()
    for at in range(0, held.shape[0], CHUNK):
        rows = slice(at, at + CHUNK)
        turned_l = dot(left_ref[rows, :], q_l, NN).astype(BF16)
        turned_c = dot(own_ref[rows, :], q_c, NN).astype(BF16)
        turned_r = dot(right_ref[rows, :], q_r, NN).astype(BF16)
        met_l = jnp.concatenate([turned_l, turned_c[:, :HALF]], axis=1)
        met_r = jnp.concatenate([turned_c[:, HALF:], turned_r], axis=1)
        held[rows, :HALF] = dot(met_l, v_l, NN).astype(BF16)
        held[rows, HALF:] = dot(met_r, v_r, NN).astype(BF16)

    (turn,) = polars([gram], [sign_of(orient_ref[2], swap)])
    turn = jnp.where(swap == 1, jnp.concatenate([turn[:, HALF:], turn[:, :HALF]], axis=1), turn)
    for at in range(0, held.shape[0], CHUNK):
        rows = slice(at, at + CHUNK)
        out_ref[rows, :] = dot(held[rows, :], turn, NN).astype(BF16)
    squares = jnp.sum(turn.astype(F32) * fine(gram, turn, NN), axis=0, keepdims=True)
    rms_ref[...] = jnp.sqrt(jnp.maximum(squares, 0.0) / total_rows)


def call(kernel, outs, spaces, operands, micros, scratch=(), megabytes=8):
    space = {"s": pltpu.SMEM, "v": pltpu.VMEM, "a": pl.ANY}
    return pl.pallas_call(
        kernel,
        out_shape=outs,
        in_specs=[pl.BlockSpec(memory_space=space[name]) for name in spaces],
        out_specs=jax.tree.map(lambda _: pl.BlockSpec(memory_space=pltpu.VMEM), outs),
        scratch_shapes=scratch,
        compiler_params=pltpu.CompilerParams(vmem_limit_bytes=megabytes << 20),
        cost_estimate=pl.CostEstimate(flops=micros * 10**9, bytes_accessed=0, transcendentals=0),
    )(*operands)


def per_device(snapshots, orient):
    rows_axis, pairs = lax.axis_size("rows"), lax.axis_size("cols")
    z_size = rows_axis // Y_SIZE
    along_y = [[z * Y_SIZE + y for y in range(Y_SIZE)] for z in range(z_size)]
    along_z = [[z * Y_SIZE + y for z in range(z_size)] for y in range(Y_SIZE)]
    ring = pair_ring(pairs)
    forward = [(ring[at - 1], ring[at]) for at in range(pairs)]
    backward = [(target, source) for source, target in forward]
    shape = jax.ShapeDtypeStruct
    height = snapshots.shape[0]
    pair = lax.axis_index("cols").reshape(1)
    table = jnp.asarray(routing(pairs))
    orient = orient.reshape(-1)

    def swapped(value, count, groups):
        return lax.all_to_all(value.reshape(count, -1, HALF), "rows", 0, 0, axis_index_groups=groups, tiled=True)

    with jax.named_scope("neighbours"):
        left = lax.ppermute(snapshots, "cols", forward)
        right = lax.ppermute(snapshots, "cols", backward)
    with jax.named_scope("own_gram"):
        piece, step = 2 * HALF // z_size, 3 * HALF // z_size
        gram = call(
            own_gram_kernel, shape((z_size, piece + 8, HALF), F32), "v", (snapshots,), 1
        )
        gram = swapped(gram, z_size, along_z)
    left, right, gram = lax.optimization_barrier((left, right, gram))
    with jax.named_scope("sum_y"):
        both = call(
            cross_gram_kernel, shape((Y_SIZE, 3 * HALF + 2 * (piece + 8), HALF), BF16), "vvvv",
            (left, snapshots, right, gram), 2,
        )
        both = swapped(both, Y_SIZE, along_y)
        both, diagonal = call(
            summed_y_kernel, (shape((z_size, step + piece, HALF), F32), shape((8, HALF), F32)), "v", (both,), 1
        )
    both, orient = lax.optimization_barrier((both, orient))
    with jax.named_scope("neighbours"):
        below = lax.ppermute(orient, "cols", [(c - 1, c) for c in range(1, pairs)])
        above = lax.ppermute(orient, "cols", [(c, c - 1) for c in range(1, pairs)])
    with jax.named_scope("sum_z"):
        both = swapped(both, z_size, along_z)
        cross, gram = call(
            summed_z_kernel, (shape((z_size, step, HALF), F32), shape((2 * HALF, HALF), F32)), "v", (both,), 1
        )
    cross, gram, below, above = lax.optimization_barrier((cross, gram, below, above))
    with jax.named_scope("gather_z"):
        cross = swapped(cross, z_size, along_z).reshape(-1, HALF)
    with jax.named_scope("first_round"):
        sent = shape((4 * HALF, HALF), BF16)
        back, ahead, mid = call(
            first_round_kernel, (sent, sent, shape((HALF, HALF), F32)), "sssvv",
            (pair, table, orient, gram, diagonal), 9,
        )
    with jax.named_scope("neighbours"):
        from_left = lax.ppermute(ahead, "cols", forward)
        from_right = lax.ppermute(back, "cols", backward)
    cross, from_left, from_right = lax.optimization_barrier((cross, from_left, from_right))
    with jax.named_scope("gather_y"):
        cross = call(
            half_turned_kernel, shape((Y_SIZE, 3 * QUARTER, HALF), F32), "vvv", (cross, from_left, from_right), 1
        )
        cross = swapped(cross, Y_SIZE, along_y)
    with jax.named_scope("rounds"):
        operands = (cross, from_left, back, ahead, from_right, mid, left, snapshots, right)
        rotated, column_rms = call(
            functools.partial(rounds_kernel, height * rows_axis),
            (shape(snapshots.shape, BF16), shape((1, 2 * HALF), F32)),
            "sssss" + "a" * len(operands),
            (pair, table, orient, below, above, *operands),
            21,
            [pltpu.VMEM(value.shape, value.dtype) for value in operands]
            + [pltpu.VMEM(snapshots.shape, BF16), pltpu.SemaphoreType.DMA((len(operands),))],
            megabytes=52,
        )
    return rotated, column_rms.reshape(-1)


def solution(mesh):
    in_specs = (P("rows", "cols"), P(None, "cols"))
    out_specs = (P("rows", "cols"), P("cols"))
    return jax.shard_map(
        per_device, mesh=mesh, in_specs=in_specs, out_specs=out_specs, check_vma=False
    )
```

```python
import functools

import jax
import jax.numpy as jnp
import numpy as np
from jax import lax
from jax.experimental import pallas as pl
from jax.experimental.pallas import tpu as pltpu
from jax.sharding import PartitionSpec as P

POLAR_ITERS = 12
Y_SIZE = 4
HALF = 128
QUARTER = 2 * HALF // Y_SIZE
CHUNK = 512
F32 = jnp.float32
BF16 = jnp.bfloat16
NT = (((1,), (1,)), ((), ()))
NN = (((1,), (0,)), ((), ()))
TN = (((0,), (0,)), ((), ()))


def pair_ring(count):
    return list(range(0, count, 2)) + list(range(count - 1, 0, -2))


def moved(top, bottom):
    count = len(top)
    new_top = [top[0], bottom[0]] + top[1 : count - 1]
    new_bottom = bottom[1:] + [top[count - 1]]
    return new_top, new_bottom


def routing(count):
    ring = pair_ring(count)
    place = {pair: at for at, pair in enumerate(ring)}
    top, bottom = [(c, 0) for c in range(count)], [(c, 1) for c in range(count)]
    top_1, bottom_1 = moved(top, bottom)
    ends = [{top_1[m][0]: (0, top_1[m][1]), bottom_1[m][0]: (1, bottom_1[m][1])} for m in range(count)]
    top_2, bottom_2 = moved([(m, 0) for m in range(count)], [(m, 1) for m in range(count)])
    rows = []
    for c in range(count):
        left, right = ring[place[c] - 1], ring[(place[c] + 1) % count]
        edge_l = next(m for m in range(count) if set(ends[m]) == {left, c})
        edge_r = next(m for m in range(count) if set(ends[m]) == {right, c})
        swap_2 = int(top_2[c][0] == edge_r)
        take_l, take_r = (bottom_2[c], top_2[c]) if swap_2 else (top_2[c], bottom_2[c])
        assert (take_l[0], take_r[0]) == (edge_l, edge_r)
        flip_l, flip_r = ends[edge_l][c][0] == 0, ends[edge_r][c][0] == 1
        rows.append([
            left, right, edge_l, edge_r,
            ends[edge_l][left][1], ends[edge_l][c][1], ends[edge_r][c][1], ends[edge_r][right][1],
            int(flip_l), int(flip_r),
            int(take_l[1] == ends[edge_l][c][0]), int(take_r[1] == ends[edge_r][right][0]),
            swap_2,
        ])
    return np.array(rows, np.int32)


def dot(left, right, dims):
    return lax.dot_general(left, right, dims, preferred_element_type=F32)


def split(value):
    high = value.astype(BF16)
    return high, (value - high.astype(F32)).astype(BF16)


def fine(left, right, dims):
    if left.dtype == BF16:
        high, low = split(right)
        return dot(left, high, dims) + dot(left, low, dims)
    high, low = split(left)
    return dot(high, right, dims) + dot(low, right, dims)


def triangle(shape):
    return lax.broadcasted_iota(jnp.int32, shape, 0), lax.broadcasted_iota(jnp.int32, shape, 1)


def own_gram_kernel(own_ref, out_ref):
    total = dot(own_ref[...], own_ref[...], TN)
    first, apart, second = total[:HALF, :HALF], total[:HALF, HALF:], total[HALF:, HALF:]
    row, column = triangle(first.shape)
    diagonal = jnp.sum(jnp.where(row == column, second, 0.0), axis=0, keepdims=True)
    packed = jnp.concatenate([jnp.where(row <= column, first, second), apart], axis=0)
    pieces, rows = out_ref.shape[0], out_ref.shape[1] - 16
    for at in range(pieces):
        out_ref[at, :rows] = packed[at * rows : (at + 1) * rows].astype(BF16)
        out_ref[at, rows:] = jnp.broadcast_to(diagonal, (16, HALF)).astype(BF16)


def cross_gram_kernel(left_ref, own_ref, right_ref, gram_ref, out_ref):
    per_device, piece = 3 * HALF, gram_ref.shape[1] - 16
    total = jnp.sum(gram_ref[...].astype(F32), axis=0)[: piece + 8]
    high = total.astype(BF16).astype(F32)
    low = total - high
    extra = jnp.concatenate([high[:piece], low[:piece], high[piece:], low[piece:]], axis=0).astype(BF16)
    for at in range(out_ref.shape[0]):
        out_ref[at, per_device:] = extra
    pairs = (own_ref, left_ref), (own_ref, right_ref), (left_ref, right_ref)
    for at, (one, two) in enumerate(pairs):
        gram = dot(one[...], two[...], TN).astype(BF16)
        for y in range(out_ref.shape[0]):
            for half in range(2):
                row = at * HALF + half * QUARTER
                out_ref[y, row : row + QUARTER] = gram[y * QUARTER : (y + 1) * QUARTER, half * HALF : (half + 1) * HALF]


def summed_y_kernel(both_ref, out_ref, diagonal_ref):
    count, per_device = out_ref.shape[0], 3 * HALF
    step = per_device // count
    piece = out_ref.shape[1] - step
    cross = sum(both_ref[y, :per_device].astype(F32) for y in range(Y_SIZE))
    extra = sum(both_ref[y, per_device:].astype(F32) for y in range(Y_SIZE))
    gram = extra[:piece] + extra[piece : 2 * piece]
    diagonal_ref[...] = extra[2 * piece : 2 * piece + 8] + extra[2 * piece + 8 :]
    for at in range(count):
        out_ref[at, :step] = cross[at * step : (at + 1) * step]
        out_ref[at, step:] = gram


def summed_z_kernel(both_ref, out_ref, gram_ref):
    count, step = out_ref.shape[:2]
    piece = both_ref.shape[1] - step
    cross = jnp.sum(both_ref[:, :step], axis=0)
    for at in range(count):
        out_ref[at] = cross
        gram_ref[at * piece : (at + 1) * piece] = both_ref[at, step:]


def unpacked(packed_ref, diagonal):
    both, apart = packed_ref[:HALF, :], packed_ref[HALF:, :]
    row, column = triangle(both.shape)
    turned = both.T
    first = jnp.where(row <= column, both, turned)
    second = jnp.where(row == column, diagonal, jnp.where(row > column, both, turned))
    return joined(first, apart, second)


def half_turned_kernel(cross_ref, from_left_ref, from_right_ref, out_ref):
    for at, q_ref in enumerate((from_left_ref, from_right_ref, from_right_ref)):
        row = at * HALF
        gram = jnp.concatenate([cross_ref[row : row + QUARTER, :], cross_ref[row + QUARTER : row + HALF, :]], axis=1)
        value = fine(gram, q_ref[: 2 * HALF, :], NN)
        for y in range(out_ref.shape[0]):
            out_ref[y, at * QUARTER : (at + 1) * QUARTER] = value


def polar_starts(grams, signs):
    order = 2 * HALF
    row, column = triangle((order, order))
    apart = (row < HALF) != (column < HALF)
    starts = []
    for gram, sign in zip(grams, signs):
        trace_mean = jnp.sum(jnp.where(row == column, gram, 0.0)) / order + 1e-06
        upper = jnp.where(row < column, gram, 0.0) / trace_mean
        upper = jnp.where(apart, sign * upper, upper)
        starts.append(jnp.where(row == column, 1.0, 0.5 * (upper - upper.T)))
    return starts


def cubed(iterate):
    high, low = split(iterate)
    square = dot(high, high, NT) + dot(high, low, NT) + dot(low, high, NT)
    sq_high, sq_low = split(square)
    return dot(sq_high, high, NN) + dot(sq_low, high, NN) + dot(sq_high, low, NN)


def first_step(start):
    inverse = lax.rsqrt(jnp.sum(start * start))
    return inverse * (1.5 * start - (0.5 * inverse * inverse) * cubed(start))


def polars(grams, signs):
    iterates = [first_step(start) for start in polar_starts(grams, signs)]
    for _ in range(POLAR_ITERS - 1):
        iterates = [1.5 * iterate - 0.5 * cubed(iterate) for iterate in iterates]
    return [iterate.astype(BF16) for iterate in iterates]


def half_of(value, which):
    return jnp.where(which == 1, value[:, HALF:], value[:, :HALF])


def joined(top_left, top_right, bottom_right):
    top = jnp.concatenate([top_left, top_right], axis=1)
    bottom = jnp.concatenate([top_right.T, bottom_right], axis=1)
    return jnp.concatenate([top, bottom], axis=0)


def sign_of(flag, flip):
    return (1 - 2 * (flag ^ flip)).astype(F32)


def first_round_kernel(pair_ref, table_ref, orient_ref, gram_ref, diagonal_ref, back_ref, ahead_ref, mid_ref):
    pair = pair_ref[0]
    gram = unpacked(gram_ref, diagonal_ref[:1, :])
    (turn,) = polars([gram], [sign_of(orient_ref[0], 0)])
    q_c = jnp.concatenate([half_of(turn, table_ref[pair, 5]), half_of(turn, table_ref[pair, 6])], axis=1)
    after = fine(q_c, fine(gram, q_c, NN), TN)
    for ref, half in ((back_ref, slice(0, HALF)), (ahead_ref, slice(HALF, 2 * HALF))):
        high, low = split(after[half, half])
        ref[: 2 * HALF, :] = q_c[:, half]
        ref[2 * HALF : 3 * HALF, :] = high
        ref[3 * HALF :, :] = low
    mid_ref[...] = after[:HALF, HALF:]


def rounds_kernel(
    total_rows, pair_ref, table_ref, orient_ref, below_ref, above_ref,
    *rest,
):
    sources, (out_ref, rms_ref), (*kept, held, arrived) = rest[:9], rest[9:11], rest[11:]
    copies = [pltpu.make_async_copy(source, place, arrived.at[at]) for at, (source, place) in enumerate(zip(sources, kept))]
    for copy in copies[:6]:
        copy.start()
    gram_ref, from_left_ref, back_ref, ahead_ref, from_right_ref, mid_ref, left_ref, own_ref, right_ref = kept
    pair = pair_ref[0]
    look = lambda at: table_ref[pair, at]
    edge_l, edge_r, flip_l, flip_r, take_l, take_r, swap = (look(at) for at in (2, 3, 8, 9, 10, 11, 12))
    of_edge = lambda edge: jnp.where(edge < pair, below_ref[1], jnp.where(edge > pair, above_ref[1], orient_ref[1]))

    for copy in copies[:6]:
        copy.wait()
    for copy in copies[6:]:
        copy.start()
    c_l, c_r, l_r = (
        jnp.concatenate([gram_ref[y, at * QUARTER : (at + 1) * QUARTER] for y in range(Y_SIZE)], axis=0) for at in range(3)
    )
    q_l, q_cl, q_cr, q_r = (ref[: 2 * HALF, :] for ref in (from_left_ref, back_ref, ahead_ref, from_right_ref))
    d_l, d_cl, d_cr, d_r = (
        ref[2 * HALF : 3 * HALF, :].astype(F32) + ref[3 * HALF :, :].astype(F32)
        for ref in (from_left_ref, back_ref, ahead_ref, from_right_ref)
    )
    q_c = jnp.concatenate([q_cl, q_cr], axis=1)
    met = fine(q_c, jnp.concatenate([c_l, c_r], axis=1), TN)
    gram_l = joined(d_l, met[:HALF, :HALF].T, d_cl)
    gram_r = joined(d_cr, met[HALF:, HALF:], d_r)
    cross = jnp.concatenate([
        jnp.concatenate([met[HALF:, :HALF].T, fine(q_l, l_r, TN)], axis=1),
        jnp.concatenate([mid_ref[...], met[:HALF, HALF:]], axis=1),
    ], axis=0)

    e_l, e_r = polars([gram_l, gram_r], [sign_of(of_edge(edge_l), flip_l), sign_of(of_edge(edge_r), flip_r)])
    v_l, v_r = half_of(e_l, take_l), half_of(e_r, take_r)
    by_l = fine(gram_l, v_l, NN)
    by_r = fine(jnp.concatenate([cross, gram_r], axis=0), v_r, NN)
    top = fine(v_l, jnp.concatenate([by_l, by_r[: 2 * HALF]], axis=1), TN)
    gram = joined(top[:, :HALF], top[:, HALF:], fine(v_r, by_r[2 * HALF :], TN))

    for copy in copies[6:]:
        copy.wait()
    for at in range(0, held.shape[0], CHUNK):
        rows = slice(at, at + CHUNK)
        turned_l = dot(left_ref[rows, :], q_l, NN).astype(BF16)
        turned_c = dot(own_ref[rows, :], q_c, NN).astype(BF16)
        turned_r = dot(right_ref[rows, :], q_r, NN).astype(BF16)
        met_l = jnp.concatenate([turned_l, turned_c[:, :HALF]], axis=1)
        met_r = jnp.concatenate([turned_c[:, HALF:], turned_r], axis=1)
        held[rows, :HALF] = dot(met_l, v_l, NN).astype(BF16)
        held[rows, HALF:] = dot(met_r, v_r, NN).astype(BF16)

    (turn,) = polars([gram], [sign_of(orient_ref[2], swap)])
    turn = jnp.where(swap == 1, jnp.concatenate([turn[:, HALF:], turn[:, :HALF]], axis=1), turn)
    for at in range(0, held.shape[0], CHUNK):
        rows = slice(at, at + CHUNK)
        out_ref[rows, :] = dot(held[rows, :], turn, NN).astype(BF16)
    squares = jnp.sum(turn.astype(F32) * fine(gram, turn, NN), axis=0, keepdims=True)
    rms_ref[...] = jnp.sqrt(jnp.maximum(squares, 0.0) / total_rows)


def call(kernel, outs, spaces, operands, micros, scratch=(), megabytes=8):
    space = {"s": pltpu.SMEM, "v": pltpu.VMEM, "a": pl.ANY}
    return pl.pallas_call(
        kernel,
        out_shape=outs,
        in_specs=[pl.BlockSpec(memory_space=space[name]) for name in spaces],
        out_specs=jax.tree.map(lambda _: pl.BlockSpec(memory_space=pltpu.VMEM), outs),
        scratch_shapes=scratch,
        compiler_params=pltpu.CompilerParams(vmem_limit_bytes=megabytes << 20),
        cost_estimate=pl.CostEstimate(flops=micros * 10**9, bytes_accessed=0, transcendentals=0),
    )(*operands)


def per_device(snapshots, orient):
    rows_axis, pairs = lax.axis_size("rows"), lax.axis_size("cols")
    z_size = rows_axis // Y_SIZE
    along_y = [[z * Y_SIZE + y for y in range(Y_SIZE)] for z in range(z_size)]
    along_z = [[z * Y_SIZE + y for z in range(z_size)] for y in range(Y_SIZE)]
    ring = pair_ring(pairs)
    forward = [(ring[at - 1], ring[at]) for at in range(pairs)]
    backward = [(target, source) for source, target in forward]
    shape = jax.ShapeDtypeStruct
    height = snapshots.shape[0]
    pair = lax.axis_index("cols").reshape(1)
    table = jnp.asarray(routing(pairs))
    orient = orient.reshape(-1)

    def swapped(value, count, groups):
        return lax.all_to_all(value.reshape(count, -1, HALF), "rows", 0, 0, axis_index_groups=groups, tiled=True)

    with jax.named_scope("neighbours"):
        left = lax.ppermute(snapshots, "cols", forward)
        right = lax.ppermute(snapshots, "cols", backward)
    with jax.named_scope("own_gram"):
        piece, step = 2 * HALF // z_size, 3 * HALF // z_size
        gram = call(
            own_gram_kernel, shape((z_size, piece + 16, HALF), BF16), "v", (snapshots,), 1
        )
        gram = swapped(gram, z_size, along_z)
    left, right, gram = lax.optimization_barrier((left, right, gram))
    with jax.named_scope("sum_y"):
        both = call(
            cross_gram_kernel, shape((Y_SIZE, 3 * HALF + 2 * (piece + 8), HALF), BF16), "vvvv",
            (left, snapshots, right, gram), 2,
        )
        both = swapped(both, Y_SIZE, along_y)
        both, diagonal = call(
            summed_y_kernel, (shape((z_size, step + piece, HALF), F32), shape((8, HALF), F32)), "v", (both,), 1
        )
    both, orient = lax.optimization_barrier((both, orient))
    with jax.named_scope("neighbours"):
        below = lax.ppermute(orient, "cols", [(c - 1, c) for c in range(1, pairs)])
        above = lax.ppermute(orient, "cols", [(c, c - 1) for c in range(1, pairs)])
    with jax.named_scope("sum_z"):
        both = swapped(both, z_size, along_z)
        cross, gram = call(
            summed_z_kernel, (shape((z_size, step, HALF), F32), shape((2 * HALF, HALF), F32)), "v", (both,), 1
        )
    cross, gram, below, above = lax.optimization_barrier((cross, gram, below, above))
    with jax.named_scope("gather_z"):
        cross = swapped(cross, z_size, along_z).reshape(-1, HALF)
    with jax.named_scope("first_round"):
        sent = shape((4 * HALF, HALF), BF16)
        back, ahead, mid = call(
            first_round_kernel, (sent, sent, shape((HALF, HALF), F32)), "sssvv",
            (pair, table, orient, gram, diagonal), 9,
        )
    with jax.named_scope("neighbours"):
        from_left = lax.ppermute(ahead, "cols", forward)
        from_right = lax.ppermute(back, "cols", backward)
    cross, from_left, from_right = lax.optimization_barrier((cross, from_left, from_right))
    with jax.named_scope("gather_y"):
        cross = call(
            half_turned_kernel, shape((Y_SIZE, 3 * QUARTER, HALF), F32), "vvv", (cross, from_left, from_right), 1
        )
        cross = swapped(cross, Y_SIZE, along_y)
    with jax.named_scope("rounds"):
        operands = (cross, from_left, back, ahead, from_right, mid, left, snapshots, right)
        rotated, column_rms = call(
            functools.partial(rounds_kernel, height * rows_axis),
            (shape(snapshots.shape, BF16), shape((1, 2 * HALF), F32)),
            "sssss" + "a" * len(operands),
            (pair, table, orient, below, above, *operands),
            21,
            [pltpu.VMEM(value.shape, value.dtype) for value in operands]
            + [pltpu.VMEM(snapshots.shape, BF16), pltpu.SemaphoreType.DMA((len(operands),))],
            megabytes=52,
        )
    return rotated, column_rms.reshape(-1)


def solution(mesh):
    in_specs = (P("rows", "cols"), P(None, "cols"))
    out_specs = (P("rows", "cols"), P("cols"))
    return jax.shard_map(
        per_device, mesh=mesh, in_specs=in_specs, out_specs=out_specs, check_vma=False
    )
```

```python
import functools

import jax
import jax.numpy as jnp
import numpy as np
from jax import lax
from jax.experimental import pallas as pl
from jax.experimental.pallas import tpu as pltpu
from jax.sharding import PartitionSpec as P

POLAR_ITERS = 12
Y_SIZE = 4
HALF = 128
QUARTER = 2 * HALF // Y_SIZE
CHUNK = 512
F32 = jnp.float32
BF16 = jnp.bfloat16
NT = (((1,), (1,)), ((), ()))
NN = (((1,), (0,)), ((), ()))
TN = (((0,), (0,)), ((), ()))


def pair_ring(count):
    return list(range(0, count, 2)) + list(range(count - 1, 0, -2))


def moved(top, bottom):
    count = len(top)
    new_top = [top[0], bottom[0]] + top[1 : count - 1]
    new_bottom = bottom[1:] + [top[count - 1]]
    return new_top, new_bottom


def routing(count):
    ring = pair_ring(count)
    place = {pair: at for at, pair in enumerate(ring)}
    top, bottom = [(c, 0) for c in range(count)], [(c, 1) for c in range(count)]
    top_1, bottom_1 = moved(top, bottom)
    ends = [{top_1[m][0]: (0, top_1[m][1]), bottom_1[m][0]: (1, bottom_1[m][1])} for m in range(count)]
    top_2, bottom_2 = moved([(m, 0) for m in range(count)], [(m, 1) for m in range(count)])
    rows = []
    for c in range(count):
        left, right = ring[place[c] - 1], ring[(place[c] + 1) % count]
        edge_l = next(m for m in range(count) if set(ends[m]) == {left, c})
        edge_r = next(m for m in range(count) if set(ends[m]) == {right, c})
        swap_2 = int(top_2[c][0] == edge_r)
        take_l, take_r = (bottom_2[c], top_2[c]) if swap_2 else (top_2[c], bottom_2[c])
        assert (take_l[0], take_r[0]) == (edge_l, edge_r)
        flip_l, flip_r = ends[edge_l][c][0] == 0, ends[edge_r][c][0] == 1
        rows.append([
            left, right, edge_l, edge_r,
            ends[edge_l][left][1], ends[edge_l][c][1], ends[edge_r][c][1], ends[edge_r][right][1],
            int(flip_l), int(flip_r),
            int(take_l[1] == ends[edge_l][c][0]), int(take_r[1] == ends[edge_r][right][0]),
            swap_2,
        ])
    return np.array(rows, np.int32)


def dot(left, right, dims):
    return lax.dot_general(left, right, dims, preferred_element_type=F32)


def split(value):
    high = value.astype(BF16)
    return high, (value - high.astype(F32)).astype(BF16)


def fine(left, right, dims):
    if left.dtype == BF16:
        high, low = split(right)
        return dot(left, high, dims) + dot(left, low, dims)
    high, low = split(left)
    return dot(high, right, dims) + dot(low, right, dims)


def triangle(shape):
    return lax.broadcasted_iota(jnp.int32, shape, 0), lax.broadcasted_iota(jnp.int32, shape, 1)


def own_gram_kernel(own_ref, out_ref):
    total = dot(own_ref[...], own_ref[...], TN)
    first, apart, second = total[:HALF, :HALF], total[:HALF, HALF:], total[HALF:, HALF:]
    row, column = triangle(first.shape)
    diagonal = jnp.sum(jnp.where(row == column, second, 0.0), axis=0, keepdims=True)
    packed = jnp.concatenate([jnp.where(row <= column, first, second), apart], axis=0)
    pieces, rows = out_ref.shape[0], out_ref.shape[1] - 8
    for at in range(pieces):
        out_ref[at, :rows] = packed[at * rows : (at + 1) * rows]
        out_ref[at, rows:] = jnp.broadcast_to(diagonal, (8, HALF))


def cross_gram_kernel(left_ref, own_ref, right_ref, gram_ref, out_ref):
    per_device, piece = 3 * HALF, gram_ref.shape[1] - 8
    total = jnp.sum(gram_ref[...], axis=0)
    high = total.astype(BF16).astype(F32)
    low = total - high
    extra = jnp.concatenate([high[:piece], low[:piece], high[piece:], low[piece:]], axis=0).astype(BF16)
    for at in range(out_ref.shape[0]):
        out_ref[at, per_device:] = extra
    pairs = (own_ref, left_ref), (own_ref, right_ref), (left_ref, right_ref)
    for at, (one, two) in enumerate(pairs):
        gram = dot(one[...], two[...], TN).astype(BF16)
        for y in range(out_ref.shape[0]):
            for half in range(2):
                row = at * HALF + half * QUARTER
                out_ref[y, row : row + QUARTER] = gram[y * QUARTER : (y + 1) * QUARTER, half * HALF : (half + 1) * HALF]


def summed_y_kernel(both_ref, out_ref, diagonal_ref):
    count, per_device = out_ref.shape[0], 3 * HALF
    step = per_device // count
    piece = out_ref.shape[1] - step
    cross = sum(both_ref[y, :per_device].astype(F32) for y in range(Y_SIZE))
    extra = sum(both_ref[y, per_device:].astype(F32) for y in range(Y_SIZE))
    gram = extra[:piece] + extra[piece : 2 * piece]
    diagonal_ref[...] = extra[2 * piece : 2 * piece + 8] + extra[2 * piece + 8 :]
    for at in range(count):
        out_ref[at, :step] = cross[at * step : (at + 1) * step]
        out_ref[at, step:] = gram


def summed_z_kernel(both_ref, out_ref, gram_ref):
    count, step = out_ref.shape[:2]
    piece = both_ref.shape[1] - step
    cross = jnp.sum(both_ref[:, :step], axis=0)
    for at in range(count):
        out_ref[at] = cross
        gram_ref[at * piece : (at + 1) * piece] = both_ref[at, step:]


def unpacked(packed_ref, diagonal):
    both, apart = packed_ref[:HALF, :], packed_ref[HALF:, :]
    row, column = triangle(both.shape)
    turned = both.T
    first = jnp.where(row <= column, both, turned)
    second = jnp.where(row == column, diagonal, jnp.where(row > column, both, turned))
    return joined(first, apart, second)


def half_turned_kernel(cross_ref, from_left_ref, from_right_ref, out_ref):
    for at, q_ref in enumerate((from_left_ref, from_right_ref, from_right_ref)):
        row = at * HALF
        gram = jnp.concatenate([cross_ref[row : row + QUARTER, :], cross_ref[row + QUARTER : row + HALF, :]], axis=1)
        value = fine(gram, q_ref[: 2 * HALF, :], NN)
        for y in range(out_ref.shape[0]):
            out_ref[y, at * QUARTER : (at + 1) * QUARTER] = value


def polar_starts(grams, signs):
    order = 2 * HALF
    row, column = triangle((order, order))
    apart = (row < HALF) != (column < HALF)
    starts = []
    for gram, sign in zip(grams, signs):
        trace_mean = jnp.sum(jnp.where(row == column, gram, 0.0)) / order + 1e-06
        upper = jnp.where(row < column, gram, 0.0) / trace_mean
        upper = jnp.where(apart, sign * upper, upper)
        starts.append(jnp.where(row == column, 1.0, 0.5 * (upper - upper.T)))
    return starts


def cubed(iterate):
    high, low = split(iterate)
    square = dot(high, high, NT) + dot(high, low, NT) + dot(low, high, NT)
    sq_high, sq_low = split(square)
    return dot(sq_high, high, NN) + dot(sq_low, high, NN) + dot(sq_high, low, NN)


def first_step(start):
    inverse = lax.rsqrt(jnp.sum(start * start))
    return inverse * (1.5 * start - (0.5 * inverse * inverse) * cubed(start))


def polars(grams, signs):
    iterates = [first_step(start) for start in polar_starts(grams, signs)]
    for _ in range(POLAR_ITERS - 1):
        iterates = [1.5 * iterate - 0.5 * cubed(iterate) for iterate in iterates]
    return [iterate.astype(BF16) for iterate in iterates]


def half_of(value, which):
    return jnp.where(which == 1, value[:, HALF:], value[:, :HALF])


def joined(top_left, top_right, bottom_right):
    top = jnp.concatenate([top_left, top_right], axis=1)
    bottom = jnp.concatenate([top_right.T, bottom_right], axis=1)
    return jnp.concatenate([top, bottom], axis=0)


def sign_of(flag, flip):
    return (1 - 2 * (flag ^ flip)).astype(F32)


def first_round_kernel(pair_ref, table_ref, orient_ref, gram_ref, diagonal_ref, back_ref, ahead_ref, mid_ref):
    pair = pair_ref[0]
    gram = unpacked(gram_ref, diagonal_ref[:1, :])
    (turn,) = polars([gram], [sign_of(orient_ref[0], 0)])
    q_c = jnp.concatenate([half_of(turn, table_ref[pair, 5]), half_of(turn, table_ref[pair, 6])], axis=1)
    after = fine(q_c, fine(gram, q_c, NN), TN)
    for ref, half in ((back_ref, slice(0, HALF)), (ahead_ref, slice(HALF, 2 * HALF))):
        high, low = split(after[half, half])
        ref[: 2 * HALF, :] = q_c[:, half]
        ref[2 * HALF : 3 * HALF, :] = high
        ref[3 * HALF :, :] = low
    mid_ref[...] = after[:HALF, HALF:]


def rounds_kernel(
    total_rows, pair_ref, table_ref, orient_ref, below_ref, above_ref,
    *rest,
):
    gram_ref, from_left_ref, back_ref, ahead_ref, from_right_ref, mid_ref = rest[:6]
    sources, (out_ref, rms_ref), (*kept, held, arrived) = rest[6:9], rest[9:11], rest[11:]
    copies = [pltpu.make_async_copy(source, place, arrived.at[at]) for at, (source, place) in enumerate(zip(sources, kept))]
    for copy in copies:
        copy.start()
    left_ref, own_ref, right_ref = kept
    pair = pair_ref[0]
    look = lambda at: table_ref[pair, at]
    edge_l, edge_r, flip_l, flip_r, take_l, take_r, swap = (look(at) for at in (2, 3, 8, 9, 10, 11, 12))
    of_edge = lambda edge: jnp.where(edge < pair, below_ref[1], jnp.where(edge > pair, above_ref[1], orient_ref[1]))

    c_l, c_r, l_r = (
        jnp.concatenate([gram_ref[y, at * QUARTER : (at + 1) * QUARTER] for y in range(Y_SIZE)], axis=0) for at in range(3)
    )
    q_l, q_cl, q_cr, q_r = (ref[: 2 * HALF, :] for ref in (from_left_ref, back_ref, ahead_ref, from_right_ref))
    d_l, d_cl, d_cr, d_r = (
        ref[2 * HALF : 3 * HALF, :].astype(F32) + ref[3 * HALF :, :].astype(F32)
        for ref in (from_left_ref, back_ref, ahead_ref, from_right_ref)
    )
    q_c = jnp.concatenate([q_cl, q_cr], axis=1)
    met = fine(q_c, jnp.concatenate([c_l, c_r], axis=1), TN)
    gram_l = joined(d_l, met[:HALF, :HALF].T, d_cl)
    gram_r = joined(d_cr, met[HALF:, HALF:], d_r)
    cross = jnp.concatenate([
        jnp.concatenate([met[HALF:, :HALF].T, fine(q_l, l_r, TN)], axis=1),
        jnp.concatenate([mid_ref[...], met[:HALF, HALF:]], axis=1),
    ], axis=0)

    e_l, e_r = polars([gram_l, gram_r], [sign_of(of_edge(edge_l), flip_l), sign_of(of_edge(edge_r), flip_r)])
    v_l, v_r = half_of(e_l, take_l), half_of(e_r, take_r)
    by_l = fine(gram_l, v_l, NN)
    by_r = fine(jnp.concatenate([cross, gram_r], axis=0), v_r, NN)
    top = fine(v_l, jnp.concatenate([by_l, by_r[: 2 * HALF]], axis=1), TN)
    gram = joined(top[:, :HALF], top[:, HALF:], fine(v_r, by_r[2 * HALF :], TN))

    for copy in copies:
        copy.wait()
    for at in range(0, held.shape[0], CHUNK):
        rows = slice(at, at + CHUNK)
        turned_l = dot(left_ref[rows, :], q_l, NN).astype(BF16)
        turned_c = dot(own_ref[rows, :], q_c, NN).astype(BF16)
        turned_r = dot(right_ref[rows, :], q_r, NN).astype(BF16)
        met_l = jnp.concatenate([turned_l, turned_c[:, :HALF]], axis=1)
        met_r = jnp.concatenate([turned_c[:, HALF:], turned_r], axis=1)
        held[rows, :HALF] = dot(met_l, v_l, NN).astype(BF16)
        held[rows, HALF:] = dot(met_r, v_r, NN).astype(BF16)

    (turn,) = polars([gram], [sign_of(orient_ref[2], swap)])
    turn = jnp.where(swap == 1, jnp.concatenate([turn[:, HALF:], turn[:, :HALF]], axis=1), turn)
    for at in range(0, held.shape[0], CHUNK):
        rows = slice(at, at + CHUNK)
        out_ref[rows, :] = dot(held[rows, :], turn, NN).astype(BF16)
    squares = jnp.sum(turn.astype(F32) * fine(gram, turn, NN), axis=0, keepdims=True)
    rms_ref[...] = jnp.sqrt(jnp.maximum(squares, 0.0) / total_rows)


def call(kernel, outs, spaces, operands, micros, scratch=(), megabytes=8):
    space = {"s": pltpu.SMEM, "v": pltpu.VMEM, "a": pl.ANY}
    return pl.pallas_call(
        kernel,
        out_shape=outs,
        in_specs=[pl.BlockSpec(memory_space=space[name]) for name in spaces],
        out_specs=jax.tree.map(lambda _: pl.BlockSpec(memory_space=pltpu.VMEM), outs),
        scratch_shapes=scratch,
        compiler_params=pltpu.CompilerParams(vmem_limit_bytes=megabytes << 20),
        cost_estimate=pl.CostEstimate(flops=micros * 10**9, bytes_accessed=0, transcendentals=0),
    )(*operands)


def per_device(snapshots, orient):
    rows_axis, pairs = lax.axis_size("rows"), lax.axis_size("cols")
    z_size = rows_axis // Y_SIZE
    along_y = [[z * Y_SIZE + y for y in range(Y_SIZE)] for z in range(z_size)]
    along_z = [[z * Y_SIZE + y for z in range(z_size)] for y in range(Y_SIZE)]
    ring = pair_ring(pairs)
    forward = [(ring[at - 1], ring[at]) for at in range(pairs)]
    backward = [(target, source) for source, target in forward]
    shape = jax.ShapeDtypeStruct
    height = snapshots.shape[0]
    pair = lax.axis_index("cols").reshape(1)
    table = jnp.asarray(routing(pairs))
    orient = orient.reshape(-1)

    def swapped(value, count, groups):
        return lax.all_to_all(value.reshape(count, -1, HALF), "rows", 0, 0, axis_index_groups=groups, tiled=True)

    with jax.named_scope("neighbours"):
        left = lax.ppermute(snapshots, "cols", forward)
        right = lax.ppermute(snapshots, "cols", backward)
    with jax.named_scope("own_gram"):
        piece, step = 2 * HALF // z_size, 3 * HALF // z_size
        gram = call(
            own_gram_kernel, shape((z_size, piece + 8, HALF), F32), "v", (snapshots,), 1
        )
        gram = swapped(gram, z_size, along_z)
    left, right, gram = lax.optimization_barrier((left, right, gram))
    with jax.named_scope("sum_y"):
        both = call(
            cross_gram_kernel, shape((Y_SIZE, 3 * HALF + 2 * (piece + 8), HALF), BF16), "vvvv",
            (left, snapshots, right, gram), 2,
        )
        both = swapped(both, Y_SIZE, along_y)
        both, diagonal = call(
            summed_y_kernel, (shape((z_size, step + piece, HALF), F32), shape((8, HALF), F32)), "v", (both,), 1
        )
    both, orient = lax.optimization_barrier((both, orient))
    with jax.named_scope("neighbours"):
        below = lax.ppermute(orient, "cols", [(c - 1, c) for c in range(1, pairs)])
        above = lax.ppermute(orient, "cols", [(c, c - 1) for c in range(1, pairs)])
    with jax.named_scope("sum_z"):
        both = swapped(both, z_size, along_z)
        cross, gram = call(
            summed_z_kernel, (shape((z_size, step, HALF), F32), shape((2 * HALF, HALF), F32)), "v", (both,), 1
        )
    cross, gram, below, above = lax.optimization_barrier((cross, gram, below, above))
    with jax.named_scope("gather_z"):
        cross = swapped(cross, z_size, along_z).reshape(-1, HALF)
    with jax.named_scope("first_round"):
        sent = shape((4 * HALF, HALF), BF16)
        back, ahead, mid = call(
            first_round_kernel, (sent, sent, shape((HALF, HALF), F32)), "sssvv",
            (pair, table, orient, gram, diagonal), 9,
        )
    with jax.named_scope("neighbours"):
        from_left = lax.ppermute(ahead, "cols", forward)
        from_right = lax.ppermute(back, "cols", backward)
    cross, from_left, from_right = lax.optimization_barrier((cross, from_left, from_right))
    with jax.named_scope("gather_y"):
        cross = call(
            half_turned_kernel, shape((Y_SIZE, 3 * QUARTER, HALF), F32), "vvv", (cross, from_left, from_right), 1
        )
        cross = swapped(cross, Y_SIZE, along_y)
    with jax.named_scope("rounds"):
        operands = (cross, from_left, back, ahead, from_right, mid)
        columns = (left, snapshots, right)
        rotated, column_rms = call(
            functools.partial(rounds_kernel, height * rows_axis),
            (shape(snapshots.shape, BF16), shape((1, 2 * HALF), F32)),
            "sssss" + "v" * len(operands) + "a" * len(columns),
            (pair, table, orient, below, above, *operands, *columns),
            21,
            [pltpu.VMEM(value.shape, value.dtype) for value in columns]
            + [pltpu.VMEM(snapshots.shape, BF16), pltpu.SemaphoreType.DMA((len(columns),))],
            megabytes=52,
        )
    return rotated, column_rms.reshape(-1)


def solution(mesh):
    in_specs = (P("rows", "cols"), P(None, "cols"))
    out_specs = (P("rows", "cols"), P("cols"))
    return jax.shard_map(
        per_device, mesh=mesh, in_specs=in_specs, out_specs=out_specs, check_vma=False
    )
```

```python
import functools

import jax
import jax.numpy as jnp
import numpy as np
from jax import lax
from jax.experimental import pallas as pl
from jax.experimental.pallas import tpu as pltpu
from jax.sharding import PartitionSpec as P

POLAR_ITERS = 12
Y_SIZE = 4
HALF = 128
QUARTER = 2 * HALF // Y_SIZE
CHUNK = 512
F32 = jnp.float32
BF16 = jnp.bfloat16
NT = (((1,), (1,)), ((), ()))
NN = (((1,), (0,)), ((), ()))
TN = (((0,), (0,)), ((), ()))


def pair_ring(count):
    return list(range(0, count, 2)) + list(range(count - 1, 0, -2))


def moved(top, bottom):
    count = len(top)
    new_top = [top[0], bottom[0]] + top[1 : count - 1]
    new_bottom = bottom[1:] + [top[count - 1]]
    return new_top, new_bottom


def routing(count):
    ring = pair_ring(count)
    place = {pair: at for at, pair in enumerate(ring)}
    top, bottom = [(c, 0) for c in range(count)], [(c, 1) for c in range(count)]
    top_1, bottom_1 = moved(top, bottom)
    ends = [{top_1[m][0]: (0, top_1[m][1]), bottom_1[m][0]: (1, bottom_1[m][1])} for m in range(count)]
    top_2, bottom_2 = moved([(m, 0) for m in range(count)], [(m, 1) for m in range(count)])
    rows = []
    for c in range(count):
        left, right = ring[place[c] - 1], ring[(place[c] + 1) % count]
        edge_l = next(m for m in range(count) if set(ends[m]) == {left, c})
        edge_r = next(m for m in range(count) if set(ends[m]) == {right, c})
        swap_2 = int(top_2[c][0] == edge_r)
        take_l, take_r = (bottom_2[c], top_2[c]) if swap_2 else (top_2[c], bottom_2[c])
        assert (take_l[0], take_r[0]) == (edge_l, edge_r)
        flip_l, flip_r = ends[edge_l][c][0] == 0, ends[edge_r][c][0] == 1
        rows.append([
            left, right, edge_l, edge_r,
            ends[edge_l][left][1], ends[edge_l][c][1], ends[edge_r][c][1], ends[edge_r][right][1],
            int(flip_l), int(flip_r),
            int(take_l[1] == ends[edge_l][c][0]), int(take_r[1] == ends[edge_r][right][0]),
            swap_2,
        ])
    return np.array(rows, np.int32)


def dot(left, right, dims):
    return lax.dot_general(left, right, dims, preferred_element_type=F32)


def split(value):
    high = value.astype(BF16)
    return high, (value - high.astype(F32)).astype(BF16)


def fine(left, right, dims):
    if left.dtype == BF16:
        high, low = split(right)
        return dot(left, high, dims) + dot(left, low, dims)
    high, low = split(left)
    return dot(high, right, dims) + dot(low, right, dims)


def triangle(shape):
    return lax.broadcasted_iota(jnp.int32, shape, 0), lax.broadcasted_iota(jnp.int32, shape, 1)


def own_gram_kernel(own_ref, out_ref):
    total = dot(own_ref[...], own_ref[...], TN)
    first, apart, second = total[:HALF, :HALF], total[:HALF, HALF:], total[HALF:, HALF:]
    row, column = triangle(first.shape)
    diagonal = jnp.sum(jnp.where(row == column, second, 0.0), axis=0, keepdims=True)
    packed = jnp.concatenate([jnp.where(row <= column, first, second), apart], axis=0)
    pieces, rows = out_ref.shape[0], out_ref.shape[1] - 8
    for at in range(pieces):
        out_ref[at, :rows] = packed[at * rows : (at + 1) * rows]
        out_ref[at, rows:] = jnp.broadcast_to(diagonal, (8, HALF))


def cross_gram_kernel(left_ref, own_ref, right_ref, gram_ref, out_ref):
    per_device, piece = 3 * HALF, gram_ref.shape[1] - 8
    total = jnp.sum(gram_ref[...], axis=0)
    high = total.astype(BF16).astype(F32)
    low = total - high
    extra = jnp.concatenate([high[:piece], low[:piece], high[piece:], low[piece:]], axis=0).astype(BF16)
    for at in range(out_ref.shape[0]):
        out_ref[at, per_device:] = extra
    pairs = (own_ref, left_ref), (own_ref, right_ref), (left_ref, right_ref)
    for at, (one, two) in enumerate(pairs):
        gram = dot(one[...], two[...], TN).astype(BF16)
        for y in range(out_ref.shape[0]):
            for half in range(2):
                row = at * HALF + half * QUARTER
                out_ref[y, row : row + QUARTER] = gram[y * QUARTER : (y + 1) * QUARTER, half * HALF : (half + 1) * HALF]


def summed_y_kernel(both_ref, out_ref, diagonal_ref):
    count, per_device = out_ref.shape[0], 3 * HALF
    step = per_device // count
    piece = out_ref.shape[1] - step
    cross = sum(both_ref[y, :per_device].astype(F32) for y in range(Y_SIZE))
    extra = sum(both_ref[y, per_device:].astype(F32) for y in range(Y_SIZE))
    gram = extra[:piece] + extra[piece : 2 * piece]
    diagonal_ref[...] = extra[2 * piece : 2 * piece + 8] + extra[2 * piece + 8 :]
    for at in range(count):
        out_ref[at, :step] = cross[at * step : (at + 1) * step]
        out_ref[at, step:] = gram


def summed_z_kernel(both_ref, out_ref, gram_ref):
    count, step = out_ref.shape[:2]
    piece = both_ref.shape[1] - step
    cross = jnp.sum(both_ref[:, :step], axis=0)
    for at in range(count):
        out_ref[at] = cross
        gram_ref[at * piece : (at + 1) * piece] = both_ref[at, step:]


def unpacked(packed_ref, diagonal):
    both, apart = packed_ref[:HALF, :], packed_ref[HALF:, :]
    row, column = triangle(both.shape)
    turned = both.T
    first = jnp.where(row <= column, both, turned)
    second = jnp.where(row == column, diagonal, jnp.where(row > column, both, turned))
    return joined(first, apart, second)


def half_turned_kernel(cross_ref, from_left_ref, from_right_ref, out_ref):
    for at, q_ref in enumerate((from_left_ref, from_right_ref, from_right_ref)):
        row = at * HALF
        gram = jnp.concatenate([cross_ref[row : row + QUARTER, :], cross_ref[row + QUARTER : row + HALF, :]], axis=1)
        value = fine(gram, q_ref[: 2 * HALF, :], NN)
        for y in range(out_ref.shape[0]):
            out_ref[y, at * QUARTER : (at + 1) * QUARTER] = value


def polar_starts(grams, signs):
    order = 2 * HALF
    row, column = triangle((order, order))
    apart = (row < HALF) != (column < HALF)
    starts = []
    for gram, sign in zip(grams, signs):
        trace_mean = jnp.sum(jnp.where(row == column, gram, 0.0)) / order + 1e-06
        upper = jnp.where(row < column, gram, 0.0) / trace_mean
        upper = jnp.where(apart, sign * upper, upper)
        starts.append(jnp.where(row == column, 1.0, 0.5 * (upper - upper.T)))
    return starts


def cubed(iterate):
    high, low = split(iterate)
    order = iterate.shape[0]
    tall = dot(jnp.concatenate([high, low], axis=0), high, NT)
    square = tall[:order] + tall[order:] + dot(high, low, NT)
    sq_high, sq_low = split(square)
    tall = dot(jnp.concatenate([sq_high, sq_low], axis=0), high, NN)
    return tall[:order] + tall[order:] + dot(sq_high, low, NN)


def first_step(start):
    inverse = lax.rsqrt(jnp.sum(start * start))
    return inverse * (1.5 * start - (0.5 * inverse * inverse) * cubed(start))


def polars(grams, signs):
    iterates = [first_step(start) for start in polar_starts(grams, signs)]
    for _ in range(POLAR_ITERS - 1):
        iterates = [1.5 * iterate - 0.5 * cubed(iterate) for iterate in iterates]
    return [iterate.astype(BF16) for iterate in iterates]


def half_of(value, which):
    return jnp.where(which == 1, value[:, HALF:], value[:, :HALF])


def joined(top_left, top_right, bottom_right):
    top = jnp.concatenate([top_left, top_right], axis=1)
    bottom = jnp.concatenate([top_right.T, bottom_right], axis=1)
    return jnp.concatenate([top, bottom], axis=0)


def sign_of(flag, flip):
    return (1 - 2 * (flag ^ flip)).astype(F32)


def first_round_kernel(pair_ref, table_ref, orient_ref, gram_ref, diagonal_ref, back_ref, ahead_ref, mid_ref):
    pair = pair_ref[0]
    gram = unpacked(gram_ref, diagonal_ref[:1, :])
    (turn,) = polars([gram], [sign_of(orient_ref[0], 0)])
    q_c = jnp.concatenate([half_of(turn, table_ref[pair, 5]), half_of(turn, table_ref[pair, 6])], axis=1)
    after = fine(q_c, fine(gram, q_c, NN), TN)
    for ref, half in ((back_ref, slice(0, HALF)), (ahead_ref, slice(HALF, 2 * HALF))):
        high, low = split(after[half, half])
        ref[: 2 * HALF, :] = q_c[:, half]
        ref[2 * HALF : 3 * HALF, :] = high
        ref[3 * HALF :, :] = low
    mid_ref[...] = after[:HALF, HALF:]


def rounds_kernel(
    total_rows, pair_ref, table_ref, orient_ref, below_ref, above_ref,
    *rest,
):
    sources, (out_ref, rms_ref), (*kept, held, arrived) = rest[:9], rest[9:11], rest[11:]
    copies = [pltpu.make_async_copy(source, place, arrived.at[at]) for at, (source, place) in enumerate(zip(sources, kept))]
    for copy in copies[:6]:
        copy.start()
    gram_ref, from_left_ref, back_ref, ahead_ref, from_right_ref, mid_ref, left_ref, own_ref, right_ref = kept
    pair = pair_ref[0]
    look = lambda at: table_ref[pair, at]
    edge_l, edge_r, flip_l, flip_r, take_l, take_r, swap = (look(at) for at in (2, 3, 8, 9, 10, 11, 12))
    of_edge = lambda edge: jnp.where(edge < pair, below_ref[1], jnp.where(edge > pair, above_ref[1], orient_ref[1]))

    for copy in copies[:6]:
        copy.wait()
    for copy in copies[6:]:
        copy.start()
    c_l, c_r, l_r = (
        jnp.concatenate([gram_ref[y, at * QUARTER : (at + 1) * QUARTER] for y in range(Y_SIZE)], axis=0) for at in range(3)
    )
    q_l, q_cl, q_cr, q_r = (ref[: 2 * HALF, :] for ref in (from_left_ref, back_ref, ahead_ref, from_right_ref))
    d_l, d_cl, d_cr, d_r = (
        ref[2 * HALF : 3 * HALF, :].astype(F32) + ref[3 * HALF :, :].astype(F32)
        for ref in (from_left_ref, back_ref, ahead_ref, from_right_ref)
    )
    q_c = jnp.concatenate([q_cl, q_cr], axis=1)
    met = fine(q_c, jnp.concatenate([c_l, c_r], axis=1), TN)
    gram_l = joined(d_l, met[:HALF, :HALF].T, d_cl)
    gram_r = joined(d_cr, met[HALF:, HALF:], d_r)
    cross = jnp.concatenate([
        jnp.concatenate([met[HALF:, :HALF].T, fine(q_l, l_r, TN)], axis=1),
        jnp.concatenate([mid_ref[...], met[:HALF, HALF:]], axis=1),
    ], axis=0)

    e_l, e_r = polars([gram_l, gram_r], [sign_of(of_edge(edge_l), flip_l), sign_of(of_edge(edge_r), flip_r)])
    v_l, v_r = half_of(e_l, take_l), half_of(e_r, take_r)
    by_l = fine(gram_l, v_l, NN)
    by_r = fine(jnp.concatenate([cross, gram_r], axis=0), v_r, NN)
    top = fine(v_l, jnp.concatenate([by_l, by_r[: 2 * HALF]], axis=1), TN)
    gram = joined(top[:, :HALF], top[:, HALF:], fine(v_r, by_r[2 * HALF :], TN))

    for copy in copies[6:]:
        copy.wait()
    for at in range(0, held.shape[0], CHUNK):
        rows = slice(at, at + CHUNK)
        turned_l = dot(left_ref[rows, :], q_l, NN).astype(BF16)
        turned_c = dot(own_ref[rows, :], q_c, NN).astype(BF16)
        turned_r = dot(right_ref[rows, :], q_r, NN).astype(BF16)
        met_l = jnp.concatenate([turned_l, turned_c[:, :HALF]], axis=1)
        met_r = jnp.concatenate([turned_c[:, HALF:], turned_r], axis=1)
        held[rows, :HALF] = dot(met_l, v_l, NN).astype(BF16)
        held[rows, HALF:] = dot(met_r, v_r, NN).astype(BF16)

    (turn,) = polars([gram], [sign_of(orient_ref[2], swap)])
    turn = jnp.where(swap == 1, jnp.concatenate([turn[:, HALF:], turn[:, :HALF]], axis=1), turn)
    for at in range(0, held.shape[0], CHUNK):
        rows = slice(at, at + CHUNK)
        out_ref[rows, :] = dot(held[rows, :], turn, NN).astype(BF16)
    squares = jnp.sum(turn.astype(F32) * fine(gram, turn, NN), axis=0, keepdims=True)
    rms_ref[...] = jnp.sqrt(jnp.maximum(squares, 0.0) / total_rows)


def call(kernel, outs, spaces, operands, micros, scratch=(), megabytes=8):
    space = {"s": pltpu.SMEM, "v": pltpu.VMEM, "a": pl.ANY}
    return pl.pallas_call(
        kernel,
        out_shape=outs,
        in_specs=[pl.BlockSpec(memory_space=space[name]) for name in spaces],
        out_specs=jax.tree.map(lambda _: pl.BlockSpec(memory_space=pltpu.VMEM), outs),
        scratch_shapes=scratch,
        compiler_params=pltpu.CompilerParams(vmem_limit_bytes=megabytes << 20),
        cost_estimate=pl.CostEstimate(flops=micros * 10**9, bytes_accessed=0, transcendentals=0),
    )(*operands)


def per_device(snapshots, orient):
    rows_axis, pairs = lax.axis_size("rows"), lax.axis_size("cols")
    z_size = rows_axis // Y_SIZE
    along_y = [[z * Y_SIZE + y for y in range(Y_SIZE)] for z in range(z_size)]
    along_z = [[z * Y_SIZE + y for z in range(z_size)] for y in range(Y_SIZE)]
    ring = pair_ring(pairs)
    forward = [(ring[at - 1], ring[at]) for at in range(pairs)]
    backward = [(target, source) for source, target in forward]
    shape = jax.ShapeDtypeStruct
    height = snapshots.shape[0]
    pair = lax.axis_index("cols").reshape(1)
    table = jnp.asarray(routing(pairs))
    orient = orient.reshape(-1)

    def swapped(value, count, groups):
        return lax.all_to_all(value.reshape(count, -1, HALF), "rows", 0, 0, axis_index_groups=groups, tiled=True)

    with jax.named_scope("neighbours"):
        left = lax.ppermute(snapshots, "cols", forward)
        right = lax.ppermute(snapshots, "cols", backward)
    with jax.named_scope("own_gram"):
        piece, step = 2 * HALF // z_size, 3 * HALF // z_size
        gram = call(
            own_gram_kernel, shape((z_size, piece + 8, HALF), F32), "v", (snapshots,), 1
        )
        gram = swapped(gram, z_size, along_z)
    left, right, gram = lax.optimization_barrier((left, right, gram))
    with jax.named_scope("sum_y"):
        both = call(
            cross_gram_kernel, shape((Y_SIZE, 3 * HALF + 2 * (piece + 8), HALF), BF16), "vvvv",
            (left, snapshots, right, gram), 2,
        )
        both = swapped(both, Y_SIZE, along_y)
        both, diagonal = call(
            summed_y_kernel, (shape((z_size, step + piece, HALF), F32), shape((8, HALF), F32)), "v", (both,), 1
        )
    both, orient = lax.optimization_barrier((both, orient))
    with jax.named_scope("neighbours"):
        below = lax.ppermute(orient, "cols", [(c - 1, c) for c in range(1, pairs)])
        above = lax.ppermute(orient, "cols", [(c, c - 1) for c in range(1, pairs)])
    with jax.named_scope("sum_z"):
        both = swapped(both, z_size, along_z)
        cross, gram = call(
            summed_z_kernel, (shape((z_size, step, HALF), F32), shape((2 * HALF, HALF), F32)), "v", (both,), 1
        )
    cross, gram, below, above = lax.optimization_barrier((cross, gram, below, above))
    with jax.named_scope("gather_z"):
        cross = swapped(cross, z_size, along_z).reshape(-1, HALF)
    with jax.named_scope("first_round"):
        sent = shape((4 * HALF, HALF), BF16)
        back, ahead, mid = call(
            first_round_kernel, (sent, sent, shape((HALF, HALF), F32)), "sssvv",
            (pair, table, orient, gram, diagonal), 9,
        )
    with jax.named_scope("neighbours"):
        from_left = lax.ppermute(ahead, "cols", forward)
        from_right = lax.ppermute(back, "cols", backward)
    cross, from_left, from_right = lax.optimization_barrier((cross, from_left, from_right))
    with jax.named_scope("gather_y"):
        cross = call(
            half_turned_kernel, shape((Y_SIZE, 3 * QUARTER, HALF), F32), "vvv", (cross, from_left, from_right), 1
        )
        cross = swapped(cross, Y_SIZE, along_y)
    with jax.named_scope("rounds"):
        operands = (cross, from_left, back, ahead, from_right, mid, left, snapshots, right)
        rotated, column_rms = call(
            functools.partial(rounds_kernel, height * rows_axis),
            (shape(snapshots.shape, BF16), shape((1, 2 * HALF), F32)),
            "sssss" + "a" * len(operands),
            (pair, table, orient, below, above, *operands),
            21,
            [pltpu.VMEM(value.shape, value.dtype) for value in operands]
            + [pltpu.VMEM(snapshots.shape, BF16), pltpu.SemaphoreType.DMA((len(operands),))],
            megabytes=52,
        )
    return rotated, column_rms.reshape(-1)


def solution(mesh):
    in_specs = (P("rows", "cols"), P(None, "cols"))
    out_specs = (P("rows", "cols"), P("cols"))
    return jax.shard_map(
        per_device, mesh=mesh, in_specs=in_specs, out_specs=out_specs, check_vma=False
    )
```
